128 devices in a mesh: row: 8 (over y, x_hi), col: 16 (over z, x_lo, core).
Axes of the slice: x: 4 (x_hi: 2, x_lo: 2; x = x_hi * 2 + x_lo), y: 4, z: 4, core: 2. Of those that a mesh axis runs over, the one named last changes fastest.
Arguments:
- activations: bfloat16 [2048, 8192], P('col', 'row'), may hold values from -6 to 6
- gradients: bfloat16 [2048, 8192], P('row', 'col'), may hold values from -6 to 6
- act_basis: bfloat16 [8192, 8192], P('row', 'col'), may hold values from -0.0625 to 0.0625
- grad_basis: bfloat16 [8192, 8192], P('col', 'row'), may hold values from -0.0625 to 0.0625
- lengths: int32 [8], replicated, may hold values from 1 to 512, 2048 in all
- seq_order: int32 [8], replicated, may hold values from 0 to 7, each once
Outputs:
- correction: float32 [8192, 8192], P('row', 'col')
The draws below stay inside these ranges and needn't reach their ends.
Inputs may be any that keep to these rules, and one draw needn't show every extreme that they name: The lengths sum to 2048, and one of them is 512. `seq_order`: each sequence number appears once.
All inputs are finite; a program needn't handle non-finite values.
Results may differ from the reference program's by a relative error of at most 0.0029.
Values may be sent and summed in bfloat16 or wider, within the bound.
A program may use at most 64 MiB of HBM per device.

```python
import math
import jax
import jax.numpy as jnp
import numpy as np
from jax import lax

DIN = 8192
DOUT = 8192
SEQS = 8
LMAX = 512
TOTAL = 2048


def block_levels(key, dims, cuts, low, largest):
    loudness = 1.0
    for axis_at, parts in cuts:
        draws = jax.random.uniform(jax.random.fold_in(jax.random.fold_in(key, 6), axis_at), (parts,), jnp.float32, low / len(cuts), largest / len(cuts))
        loudness = loudness * jnp.repeat(jnp.exp(draws), dims[axis_at] // parts).reshape((-1,) + (1,) * (len(dims) - 1 - axis_at))
    return loudness


def profile(count, total, bound, skew):
    loads = [(1 << 20) // math.isqrt(standing ** skew) + 1 for standing in range(2, count + 1)]
    spare, given = total - bound - (count - 1), [1] * (count - 1)
    while spare > 0:
        candidates = [i for i in range(count - 1) if given[i] < bound]
        mass, remaining = sum([loads[i] for i in candidates]), spare
        for i in candidates:
            more = min(bound - given[i], max(1, remaining * loads[i] // mass), spare)
            given[i] = given[i] + more
            spare = spare - more
    return np.array([bound] + given)


def uneven(key, number_of, total, reach, slope):
    if number_of == 2:
        one = jax.random.randint(key, (), max(1, total - reach), min(reach, total - 1) + 1)
        return jnp.stack([one, total - one])
    sizes = jnp.asarray(profile(number_of, total, reach, slope), jnp.int32)
    twos = (number_of - 1) // 2
    source_of, sink = sizes[1:1 + 2 * twos:2], sizes[2:2 + 2 * twos:2]
    slack = jnp.minimum(source_of - 1, reach - sink)
    shifted = jax.random.randint(jax.random.fold_in(key, 1), (twos,), 0, 1 << 20) % (slack + 1)
    sizes = sizes.at[1:1 + 2 * twos:2].set(source_of - shifted).at[2:2 + 2 * twos:2].set(sink + shifted)
    return sizes[jax.random.permutation(jax.random.fold_in(key, 2), number_of)]


def noise(stream_key, extent, spread, reach, split=(), kind=jnp.bfloat16):
    entries = spread * jax.random.normal(stream_key, extent, jnp.float32)
    if split:
        entries = entries * block_levels(stream_key, extent, split, -0.22, 0.18)
    return jnp.clip(entries, -reach, reach).astype(kind)


def setup_inputs(seed: int = 0) -> dict:
    streams_of = jax.random.split(jax.random.key(seed), 7)
    return {
        "activations": noise(streams_of[0], (TOTAL, DIN), 1.0, 6.0, ((0, 16), (1, 8))),
        "gradients": noise(streams_of[1], (TOTAL, DOUT), 1.0, 6.0, ((0, 8), (1, 16))),
        "act_basis": noise(streams_of[2], (DIN, DIN), DIN ** -0.5, 0.0625, ((0, 8), (1, 16))),
        "grad_basis": noise(streams_of[3], (DOUT, DOUT), DOUT ** -0.5, 0.0625, ((0, 16), (1, 8))),
        "lengths": uneven(streams_of[4], SEQS, TOTAL, LMAX, 2).astype(jnp.int32),
        "seq_order": jax.random.permutation(streams_of[5], SEQS).astype(jnp.int32),
    }


def reference(activations, gradients, act_basis, grad_basis, lengths, seq_order):
    rot_acts = jnp.dot(activations, act_basis, preferred_element_type=jnp.float32).astype(jnp.bfloat16)
    rot_grads = jnp.dot(gradients, grad_basis, preferred_element_type=jnp.float32).astype(jnp.bfloat16)
    padded_acts = jnp.concatenate([rot_acts, jnp.zeros((LMAX, DIN), jnp.bfloat16)], axis=0)
    padded_grads = jnp.concatenate([rot_grads, jnp.zeros((LMAX, DOUT), jnp.bfloat16)], axis=0)
    select = (seq_order[:, None] == jnp.arange(SEQS, dtype=jnp.int32)[None, :]).astype(jnp.int32)
    ordered = jnp.sum(select * lengths[None, :], axis=1).astype(jnp.int32)
    starts = (jnp.cumsum(ordered) - ordered).astype(jnp.int32)

    def add_sequence(total, number):
        start = starts[number]
        window_acts = lax.dynamic_slice_in_dim(padded_acts, start, LMAX, 0)
        window_grads = lax.dynamic_slice_in_dim(padded_grads, start, LMAX, 0)
        live_rows = (jnp.arange(LMAX, dtype=jnp.int32) < ordered[number]).astype(jnp.bfloat16)
        window_grads = window_grads * live_rows[:, None]
        tile = jnp.dot(window_grads.T, window_acts, preferred_element_type=jnp.float32)
        return total + tile * tile, None

    summed, unused = lax.scan(add_sequence, jnp.zeros((DOUT, DIN), jnp.float32), jnp.arange(SEQS, dtype=jnp.int32))
    return summed * (1.0 / TOTAL)
```

```python
import functools

import jax
import jax.numpy as jnp
from jax import lax
from jax.experimental import pallas as pl
from jax.experimental.pallas import tpu as pltpu
from jax.sharding import PartitionSpec as P

MESH = pl.DeviceIdType.MESH
SEQS = 8
TOTAL = 2048
PARTS = 2
SCALE = 2.0**28

BF16, F32 = jnp.bfloat16, jnp.float32


def encode(v):
    v = v * SCALE
    return (v * v * v).astype(BF16)


def decode(m):
    v = m.astype(F32)
    size = jnp.abs(v)
    root = jnp.exp2(jnp.log2(jnp.maximum(size, 1e-37)) * (1.0 / 3.0)) * (1.0 / SCALE)
    root = jnp.where(size > 1e-37, root, 0.0)
    return jnp.where(v < 0, -root, root)


class Place:
    def __init__(self, ring, pair, peer):
        self.ring, self.pair, self.peer = ring, pair, peer

    def to(self, dr=0, dx=0):
        return self.peer(lax.rem(self.ring + dr + 4, 4), lax.rem(self.pair + dx, 2))

    def index(self, dr=0, dx=0):
        return lax.rem(self.ring + dr + 4, 4) * 2 + lax.rem(self.pair + dx, 2)


def exchange_kernel(
    acts, grads, act_basis, grad_basis, out_a, out_g,
    ga, gg, ba, bg, pf_a, pf_g, ms_a, ms_g, ra_a, ra_g, rb_a, rb_g, mx_a, mx_g, rx_a, rx_g, fin_a, fin_g,
    send_sems, recv_sems, local_sems,
):
    row, col = lax.axis_index("row"), lax.axis_index("col")
    y, xh = row // 2, lax.rem(row, 2)
    z, xl, core = col // 4, lax.rem(col // 2, 2), lax.rem(col, 2)
    other = 1 - core
    along_z = Place(z, xl, lambda r, p: (row, r * 4 + p * 2 + core))
    along_y = Place(y, xh, lambda r, p: (r * 2 + p, col))
    sibling = (row, z * 4 + xl * 2 + other)

    copies, locals_, events = {}, [], []

    def send(name, src, dst, to):
        n = len(copies)
        copy = pltpu.make_async_remote_copy(
            src_ref=src, dst_ref=dst, send_sem=send_sems.at[n], recv_sem=recv_sems.at[n],
            device_id=to, device_id_type=MESH,
        )
        copies[name] = copy
        copy.start()

    def got(name):
        copies[name].wait_recv()

    def local(src, dst):
        copy = pltpu.make_async_copy(src, dst, local_sems.at[len(locals_)])
        locals_.append(copy)
        copy.start()
        return copy

    def at(time, step, *args):
        events.append((time, len(events), functools.partial(step, *args)))

    partners = [along_z.to(1), along_z.to(3), along_z.to(0, 1), along_y.to(1), along_y.to(3), along_y.to(0, 1), sibling]
    barrier = pltpu.get_barrier_semaphore()
    for partner in partners:
        pl.semaphore_signal(barrier, inc=1, device_id=partner, device_id_type=MESH)
    own_a = local(acts, ga.at[0, 0, core])
    own_g = local(grads, gg.at[0, 0, core])
    load_a = local(act_basis, ba)
    half_of = lambda who: pl.ds(pl.multiple_of(who * 512, 512), 512)
    load_g = local(grad_basis.at[:, half_of(core)], bg.at[core])
    pl.semaphore_wait(barrier, len(partners))

    chains = {
        "a": dict(mine=acts, g=ga, first=along_z, second=along_y, pf=pf_a, ms=ms_a, ra=ra_a, rb=rb_a, mx=mx_a, rx=rx_a, fin=fin_a),
        "g": dict(mine=grads, g=gg, first=along_y, second=along_z, pf=pf_g, ms=ms_g, ra=ra_g, rb=rb_g, mx=mx_g, rx=rx_g, fin=fin_g),
    }

    def first_sends(k):
        c = chains[k]
        mine, g, place = c["mine"], c["g"], c["first"]
        send(k + "10", mine, g.at[3, 0, core], place.to(1))
        send(k + "30", mine, g.at[1, 0, core], place.to(3))
        send(k + "01", mine, g.at[0, 1, core], place.to(0, 1))
        send(k + "s00", mine, g.at[0, 0, core], sibling)

    def swap(k, dr, dx):
        g = chains[k]["g"]
        send(f"{k}s{dr}{dx}", g.at[dr, dx, core], g.at[dr, dx, core], sibling)

    def half(k, h):
        rows = 64 if k == "a" else 128
        return pl.ds(h * rows, rows)

    def pass_on(k, dx):
        g, place = chains[k]["g"], chains[k]["first"]
        got(f"{k}1{dx}")
        send(f"{k}f1{dx}", g.at[3, dx, core, half(k, 0)], g.at[2, dx, core, half(k, 0)], place.to(1))
        got(f"{k}3{dx}")
        send(f"{k}f3{dx}", g.at[1, dx, core, half(k, 1)], g.at[2, dx, core, half(k, 1)], place.to(3))
        swap(k, 3, dx)
        swap(k, 1, dx)

    def partner_block(k):
        g, place = chains[k]["g"], chains[k]["first"]
        got(k + "01")
        send(k + "11", g.at[0, 1, core], g.at[3, 1, core], place.to(1))
        send(k + "31", g.at[0, 1, core], g.at[1, 1, core], place.to(3))
        swap(k, 0, 1)

    def opposite(k, dx):
        got(f"{k}f1{dx}")
        got(f"{k}f3{dx}")
        swap(k, 2, dx)

    def partial(k, dr, dx):
        c = chains[k]
        first, second, g = c["first"], c["second"], c["g"]
        block = first.index(dr, dx)
        part, h, i = block // 4, lax.rem(block // 2, 2), lax.rem(block, 2)

        def keep(value, base):
            for s in range(value.shape[0] // 32):
                o = base + s
                q = lax.rem(o // 2 - second.ring + 4, 4)
                x = lax.rem(o % 2 + second.pair, 2)
                piece = value[s * 32 : (s + 1) * 32]
                c["pf"][q, x, part, h, i] = piece
                c["ms"][q, x, part, h, i] = encode(piece)

        if k == "a":
            for n in range(2):
                keep(jnp.dot(g[dr, dx, n], ba[...], preferred_element_type=F32), 4 * n)
        else:
            for n in range(2):
                rows = pl.ds(n * 128, 128)
                value = jnp.dot(g[dr, dx, 0, rows], bg[0], preferred_element_type=F32)
                value += jnp.dot(g[dr, dx, 1, rows], bg[1], preferred_element_type=F32)
                keep(value, 4 * n)

    def block_pair(k, dr, dx):
        got(f"{k}s{dr}{dx}")
        partial(k, dr, dx)

    def both_sides(k, dx):
        got(f"{k}s3{dx}")
        got(f"{k}s1{dx}")

        @pl.loop(0, 2)
        def _(n):
            partial(k, 1 + 2 * n, dx)

    def part_of(k, t):
        return lax.rem(chains[k]["first"].ring // 2 + t, 2)

    def spread(k, t, x):
        c = chains[k]
        ms, ra, rb, place, p = c["ms"], c["ra"], c["rb"], c["second"], part_of(k, t)
        tag = f"{k}{t}{x}"
        send(tag + "a1", ms.at[2, x, p, 0], ra.at[x, p, 0], place.to(1))
        send(tag + "a3", ms.at[2, x, p, 1], ra.at[x, p, 1], place.to(3))
        send(tag + "b1", ms.at[1, x, p, 1], rb.at[x, p, 0, 1], place.to(1))
        send(tag + "b3", ms.at[3, x, p, 0], rb.at[x, p, 1, 0], place.to(3))

    def join(k, t, x):
        c = chains[k]
        ms, ra, rb, pf, place, p = c["ms"], c["ra"], c["rb"], c["pf"], c["second"], part_of(k, t)
        tag = f"{k}{t}{x}"
        got(tag + "a1")
        ms[1, x, p, 0] = encode(pf[1, x, p, 0] + decode(ra[x, p, 0]))
        send(tag + "c1", ms.at[1, x, p, 0], rb.at[x, p, 0, 0], place.to(1))
        got(tag + "a3")
        ms[3, x, p, 1] = encode(pf[3, x, p, 1] + decode(ra[x, p, 1]))
        send(tag + "c3", ms.at[3, x, p, 1], rb.at[x, p, 1, 1], place.to(3))

    def finish(k, t, x):
        c = chains[k]
        rb, pf, place, p = c["rb"], c["pf"], c["second"], part_of(k, t)
        tag = f"{k}{t}{x}"
        for n in ("b1", "b3", "c1", "c3"):
            got(tag + n)
        total = pf[0, x, p] + (decode(rb[x, p, 0]) + decode(rb[x, p, 1]))
        if x == 1:
            c["mx"][p] = encode(total)
            send(f"{k}{t}x", c["mx"].at[p], c["rx"].at[p], place.to(0, 1))
        else:
            pf[0, 0, p] = total

    def out_of(k):
        return out_a if k == "a" else out_g.at[core]

    def region(k, p, owner, h=None):
        if h is None:
            return out_of(k).at[p, :, :, owner]
        return out_of(k).at[p, h, :, owner]

    def rounded(k, t):
        c = chains[k]
        place, p, fin = c["second"], part_of(k, t), c["fin"]
        got(f"{k}{t}x")
        fin[p] = (c["pf"][0, 0, p] + decode(c["rx"][p])).astype(BF16)
        mine = region(k, p, place.index())
        tag = f"{k}{t}r"
        send(tag + "10", fin.at[p], mine, place.to(1))
        send(tag + "30", fin.at[p], mine, place.to(3))
        send(tag + "01", fin.at[p], mine, place.to(0, 1))
        if k == "g":
            send(tag + "s00", fin.at[p], mine, sibling)
        local(fin.at[p], mine)

    def share(k, t, dr, dx):
        if k == "g":
            there = region(k, part_of(k, t), chains[k]["second"].index(dr, dx))
            send(f"{k}{t}rs{dr}{dx}", there, there, sibling)

    def pass_rounded(k, t, dx):
        place, p = chains[k]["second"], part_of(k, t)
        tag = f"{k}{t}r"
        got(f"{tag}1{dx}")
        there = region(k, p, place.index(3, dx), 0)
        send(f"{tag}f1{dx}", there, there, place.to(1))
        got(f"{tag}3{dx}")
        there = region(k, p, place.index(1, dx), 1)
        send(f"{tag}f3{dx}", there, there, place.to(3))
        share(k, t, 3, dx)
        share(k, t, 1, dx)

    def partner_rounded(k, t):
        place, p = chains[k]["second"], part_of(k, t)
        tag = f"{k}{t}r"
        got(tag + "01")
        there = region(k, p, place.index(0, 1))
        send(tag + "11", there, there, place.to(1))
        send(tag + "31", there, there, place.to(3))
        share(k, t, 0, 1)

    def opposite_rounded(k, t, dx):
        tag = f"{k}{t}r"
        got(f"{tag}f1{dx}")
        got(f"{tag}f3{dx}")
        share(k, t, 2, dx)

    for k in "ga":
        at(0, first_sends, k)
    at(0.1, lambda: send("basis", grad_basis.at[:, half_of(other)], bg.at[core], sibling))

    def loaded():
        for copy in (own_a, own_g, load_a, load_g):
            copy.wait()
        got("basis")

    at(1.9, loaded)
    for k in "ga":
        at(2, block_pair, k, 0, 0)
        at(5, pass_on, k, 0)
        at(6, partner_block, k)
        at(7.5, both_sides, k, 0)
        at(8, block_pair, k, 0, 1)
        at(9, opposite, k, 0)
        at(10, pass_on, k, 1)
        at(11, block_pair, k, 2, 0)
        at(12, both_sides, k, 1)
        at(15, opposite, k, 1)
        at(17, block_pair, k, 2, 1)
        for t, start in ((0, 12.5), (1, 18)):
            at(start, spread, k, t, 1)
            at(start + 0.1, spread, k, t, 0)
            at(start + 3, join, k, t, 1)
            at(start + 4, join, k, t, 0)
            at(start + 7, finish, k, t, 1)
            at(start + 9, finish, k, t, 0)
            at(start + 10, rounded, k, t)
            at(start + 13, pass_rounded, k, t, 0)
            at(start + 13.5, partner_rounded, k, t)
            at(start + 15, opposite_rounded, k, t, 0)
            at(start + 16, pass_rounded, k, t, 1)
            at(start + 18, opposite_rounded, k, t, 1)
    for _, _, step in sorted(events, key=lambda e: e[:2]):
        step()
    for t in range(PARTS):
        for dr in range(4):
            for dx in range(2):
                got(f"g{t}rs{dr}{dx}")
    for copy in locals_[4:]:
        copy.wait()
    for copy in copies.values():
        copy.wait_send()


def rotate(acts, grads, act_basis, grad_basis):
    any_space = pl.BlockSpec(memory_space=pl.ANY)
    shape = (2, 2, 2, 8, 32, 512)
    per_chain = lambda *dims, dtype=BF16: [pltpu.VMEM(dims, dtype)] * 2
    return pl.pallas_call(
        exchange_kernel,
        out_shape=(jax.ShapeDtypeStruct(shape, BF16), jax.ShapeDtypeStruct((2,) + shape, BF16)),
        in_specs=[any_space] * 4,
        out_specs=(any_space, any_space),
        scratch_shapes=[
            pltpu.VMEM((4, 2, 2, 128, 1024), BF16),
            pltpu.VMEM((4, 2, 2, 256, 512), BF16),
            pltpu.VMEM((1024, 512), BF16),
            pltpu.VMEM((2, 512, 512), BF16),
            *per_chain(4, 2, 2, 2, 2, 32, 512, dtype=F32),
            *per_chain(4, 2, 2, 2, 2, 32, 512),
            *per_chain(2, 2, 2, 2, 32, 512),
            *per_chain(2, 2, 2, 2, 2, 32, 512),
            *per_chain(2, 2, 2, 32, 512),
            *per_chain(2, 2, 2, 32, 512),
            *per_chain(2, 2, 2, 32, 512),
            pltpu.SemaphoreType.DMA((160,)),
            pltpu.SemaphoreType.DMA((160,)),
            pltpu.SemaphoreType.DMA((16,)),
        ],
        compiler_params=pltpu.CompilerParams(collective_id=0, has_side_effects=True, vmem_limit_bytes=60 << 20),
        cost_estimate=pl.CostEstimate(flops=4 * 2048 * 1024 * 512, bytes_accessed=10 << 20, transcendentals=0),
    )(acts, grads, act_basis, grad_basis)


CHUNK = 256


def tiles_kernel(lengths, order, ra, rg, out, tile):
    out[...] = jnp.zeros_like(out)

    @pl.loop(0, SEQS, init_carry=jnp.int32(0))
    def _(k, start):
        end = start + lengths[order[k]]
        low, high = start // CHUNK, (end + CHUNK - 1) // CHUNK
        tile[...] = jnp.zeros_like(tile)

        @pl.loop(low, high)
        def _(n):
            rows = pl.ds(pl.multiple_of(n * CHUNK, CHUNK), CHUNK)
            at = n * CHUNK + lax.broadcasted_iota(jnp.int32, (CHUNK, 1), 0)
            live = (at >= start) & (at < end)
            a = jnp.where(live, ra[rows], 0)
            for h in range(2):
                tile[h * 512 : (h + 1) * 512] += lax.dot_general(
                    rg[h, rows], a, (((0,), (0,)), ((), ())), preferred_element_type=F32
                )

        out[...] += tile[...] * tile[...]
        return end

    out[...] = out[...] * (1.0 / TOTAL)


def tiles(lengths, order, ra, rg):
    smem, vmem = pl.BlockSpec(memory_space=pltpu.SMEM), pl.BlockSpec(memory_space=pltpu.VMEM)
    return pl.pallas_call(
        tiles_kernel,
        out_shape=jax.ShapeDtypeStruct((1024, 512), F32),
        in_specs=[smem, smem, vmem, vmem],
        out_specs=vmem,
        scratch_shapes=[pltpu.VMEM((1024, 512), F32)],
        compiler_params=pltpu.CompilerParams(vmem_limit_bytes=40 << 20),
    )(lengths, order, ra, rg)


def shards(activations, gradients, act_basis, grad_basis, lengths, seq_order):
    ra, rg = rotate(activations, gradients, act_basis, grad_basis)
    return tiles(lengths, seq_order, ra.reshape(2048, 512), rg.reshape(2, 2048, 512))


def solution(mesh):
    in_specs = (P("col", "row"), P("row", "col"), P("row", "col"), P("col", "row"), P(), P())
    return jax.shard_map(shards, mesh=mesh, in_specs=in_specs, out_specs=P("row", "col"), check_vma=False)
```

```python
import functools

import jax
import jax.numpy as jnp
from jax import lax
from jax.experimental import pallas as pl
from jax.experimental.pallas import tpu as pltpu
from jax.sharding import PartitionSpec as P

MESH = pl.DeviceIdType.MESH
SEQS = 8
TOTAL = 2048
SCALE = 2.0**28

BF16, F32 = jnp.bfloat16, jnp.float32


def encode(v):
    v = v * SCALE
    return (v * v * v).astype(BF16)


def decode(m):
    v = m.astype(F32)
    size = jnp.abs(v)
    root = jnp.exp2(jnp.log2(jnp.maximum(size, 1e-37)) * (1.0 / 3.0)) * (1.0 / SCALE)
    root = jnp.where(size > 1e-37, root, 0.0)
    return jnp.where(v < 0, -root, root)


class Place:
    def __init__(self, ring, pair, peer):
        self.ring, self.pair, self.peer = ring, pair, peer

    def to(self, dr=0, dx=0):
        return self.peer(lax.rem(self.ring + dr + 4, 4), lax.rem(self.pair + dx, 2))

    def index(self, dr=0, dx=0):
        return lax.rem(self.ring + dr + 4, 4) * 2 + lax.rem(self.pair + dx, 2)


def exchange_kernel(
    acts, grads, act_basis, grad_basis, out_a, out_g,
    ga, gg, ba, bg, pf_a, pf_g, ms_a, ms_g, ra_a, ra_g, rb_a, rb_g, mx_a, mx_g, rx_a, rx_g, fin_a, fin_g,
    send_sems, recv_sems, local_sems,
):
    row, col = lax.axis_index("row"), lax.axis_index("col")
    y, xh = row // 2, lax.rem(row, 2)
    z, xl, core = col // 4, lax.rem(col // 2, 2), lax.rem(col, 2)
    other = 1 - core
    along_z = Place(z, xl, lambda r, p: (row, r * 4 + p * 2 + core))
    along_y = Place(y, xh, lambda r, p: (r * 2 + p, col))
    sibling = (row, z * 4 + xl * 2 + other)

    copies, locals_, events = {}, [], []

    def send(name, src, dst, to):
        n = len(copies)
        copy = pltpu.make_async_remote_copy(
            src_ref=src, dst_ref=dst, send_sem=send_sems.at[n], recv_sem=recv_sems.at[n],
            device_id=to, device_id_type=MESH,
        )
        copies[name] = copy
        copy.start()

    def got(name):
        copies[name].wait_recv()

    def local(src, dst):
        copy = pltpu.make_async_copy(src, dst, local_sems.at[len(locals_)])
        locals_.append(copy)
        copy.start()
        return copy

    def at(time, step, *args):
        events.append((time, len(events), functools.partial(step, *args)))

    partners = [along_z.to(1), along_z.to(3), along_z.to(0, 1), along_y.to(1), along_y.to(3), along_y.to(0, 1), sibling]
    barrier = pltpu.get_barrier_semaphore()
    for partner in partners:
        pl.semaphore_signal(barrier, inc=1, device_id=partner, device_id_type=MESH)
    own_a = local(acts, ga.at[0, 0, core])
    own_g = local(grads, gg.at[0, 0, core])
    load_a = local(act_basis, ba)
    half_of = lambda who: pl.ds(pl.multiple_of(who * 512, 512), 512)
    load_g = local(grad_basis.at[:, half_of(core)], bg.at[core])
    pl.semaphore_wait(barrier, len(partners))

    chains = {
        "a": dict(mine=acts, g=ga, first=along_z, second=along_y, pf=pf_a, ms=ms_a, ra=ra_a, rb=rb_a, mx=mx_a, rx=rx_a, fin=fin_a),
        "g": dict(mine=grads, g=gg, first=along_y, second=along_z, pf=pf_g, ms=ms_g, ra=ra_g, rb=rb_g, mx=mx_g, rx=rx_g, fin=fin_g),
    }

    def half(k, h):
        rows = 64 if k == "a" else 128
        return pl.ds(h * rows, rows)

    def first_sends(k):
        c = chains[k]
        mine, g, place = c["mine"], c["g"], c["first"]
        for h in range(2):
            rows = half(k, h)
            send(f"{k}1{h}0", mine.at[rows], g.at[3, 0, core, rows], place.to(1))
            rows = half(k, 1 - h)
            send(f"{k}3{1 - h}0", mine.at[rows], g.at[1, 0, core, rows], place.to(3))
        for h in range(2):
            rows = half(k, h)
            send(f"{k}x{h}", mine.at[rows], g.at[0, 1, core, rows], place.to(0, 1))
        send(k + "s00", mine, g.at[0, 0, core], sibling)

    def swap(k, dr, dx):
        g = chains[k]["g"]
        send(f"{k}s{dr}{dx}", g.at[dr, dx, core], g.at[dr, dx, core], sibling)

    def pass_on(k, dx):
        g, place = chains[k]["g"], chains[k]["first"]
        rows = half(k, 0)
        got(f"{k}10{dx}")
        send(f"{k}f1{dx}", g.at[3, dx, core, rows], g.at[2, dx, core, rows], place.to(1))
        rows = half(k, 1)
        got(f"{k}31{dx}")
        send(f"{k}f3{dx}", g.at[1, dx, core, rows], g.at[2, dx, core, rows], place.to(3))

    def sides(k, dx):
        got(f"{k}11{dx}")
        swap(k, 3, dx)
        got(f"{k}30{dx}")
        swap(k, 1, dx)

    def partner_block(k, h):
        g, place = chains[k]["g"], chains[k]["first"]
        got(f"{k}x{h}")
        rows = half(k, h)
        send(f"{k}1{h}1", g.at[0, 1, core, rows], g.at[3, 1, core, rows], place.to(1))
        send(f"{k}3{h}1", g.at[0, 1, core, rows], g.at[1, 1, core, rows], place.to(3))
        if h == 1:
            swap(k, 0, 1)

    def opposite(k, dx):
        got(f"{k}f1{dx}")
        got(f"{k}f3{dx}")
        swap(k, 2, dx)

    def partial(k, dr, dx):
        c = chains[k]
        first, second, g = c["first"], c["second"], c["g"]
        p, h = lax.rem(first.ring + dr, 4), lax.rem(first.pair + dx, 2)

        def keep(value, base):
            for s in range(value.shape[0] // 32):
                o = base + s
                q = lax.rem(o // 2 - second.ring + 4, 4)
                x = lax.rem(o % 2 + second.pair, 2)
                piece = value[s * 32 : (s + 1) * 32]
                c["pf"][q, p, h, x] = piece
                c["ms"][q, p, h, x] = encode(piece)

        for n in range(2):
            if k == "a":
                value = jnp.dot(g[dr, dx, n], ba[...], preferred_element_type=F32)
            else:
                rows = pl.ds(n * 128, 128)
                value = jnp.dot(g[dr, dx, 0, rows], bg[0], preferred_element_type=F32)
                value += jnp.dot(g[dr, dx, 1, rows], bg[1], preferred_element_type=F32)
            keep(value, 4 * n)

    def block(k, dr, dx):
        got(f"{k}s{dr}{dx}")
        partial(k, dr, dx)

    def both_sides(k, dx):
        got(f"{k}s3{dx}")
        got(f"{k}s1{dx}")

        @pl.loop(0, 2)
        def _(n):
            partial(k, 1 + 2 * n, dx)

    def part_of(k, t):
        return lax.rem(chains[k]["first"].ring + t, 4)

    def spread(k, t):
        c = chains[k]
        ms, ra, rb, place, p = c["ms"], c["ra"], c["rb"], c["second"], part_of(k, t)
        tag = f"{k}{t}"
        send(tag + "a1", ms.at[2, p, 0], ra.at[p, 0], place.to(1))
        send(tag + "a3", ms.at[2, p, 1], ra.at[p, 1], place.to(3))
        send(tag + "b1", ms.at[1, p, 1], rb.at[p, 0, 1], place.to(1))
        send(tag + "b3", ms.at[3, p, 0], rb.at[p, 1, 0], place.to(3))

    def join(k, t):
        c = chains[k]
        ms, ra, rb, pf, place, p = c["ms"], c["ra"], c["rb"], c["pf"], c["second"], part_of(k, t)
        tag = f"{k}{t}"
        got(tag + "a1")
        ms[1, p, 0] = encode(pf[1, p, 0] + decode(ra[p, 0]))
        send(tag + "c1", ms.at[1, p, 0], rb.at[p, 0, 0], place.to(1))
        got(tag + "a3")
        ms[3, p, 1] = encode(pf[3, p, 1] + decode(ra[p, 1]))
        send(tag + "c3", ms.at[3, p, 1], rb.at[p, 1, 1], place.to(3))

    def finish(k, t):
        c = chains[k]
        rb, pf, mx, place, p = c["rb"], c["pf"], c["mx"], c["second"], part_of(k, t)
        tag = f"{k}{t}"
        for n in ("b1", "b3", "c1", "c3"):
            got(tag + n)
        total = pf[0, p] + (decode(rb[p, 0]) + decode(rb[p, 1]))
        mx[p] = encode(total)
        send(tag + "x", mx.at[p], c["rx"].at[p], place.to(0, 1))
        pf[0, p] = total

    def region(k, t, dr, h=slice(None)):
        out = out_a if k == "a" else out_g.at[core]
        return out.at[part_of(k, t), h, lax.rem(chains[k]["second"].ring + dr, 4)]

    def rounded(k, t):
        c = chains[k]
        place, p, fin, rx, pf = c["second"], part_of(k, t), c["fin"], c["rx"], c["pf"]
        tag = f"{k}{t}"
        got(tag + "x")
        for x in range(2):
            own = lax.rem(place.pair + x, 2)
            for h in range(2):
                fin[p, h, own] = (pf[0, p, h, x] + decode(rx[p, h, 1 - x])).astype(BF16)
        mine = region(k, t, 0)
        send(tag + "r1", fin.at[p], mine, place.to(1))
        send(tag + "r3", fin.at[p], mine, place.to(3))
        if k == "g":
            send(tag + "rs0", fin.at[p], mine, sibling)
        local(fin.at[p], mine)

    def share(k, t, dr):
        if k == "g":
            send(f"{k}{t}rs{dr}", region(k, t, dr), region(k, t, dr), sibling)

    def pass_rounded(k, t):
        place, tag = chains[k]["second"], f"{k}{t}"
        got(tag + "r1")
        send(tag + "rf1", region(k, t, 3, 0), region(k, t, 3, 0), place.to(1))
        got(tag + "r3")
        send(tag + "rf3", region(k, t, 1, 1), region(k, t, 1, 1), place.to(3))
        share(k, t, 3)
        share(k, t, 1)

    def opposite_rounded(k, t):
        got(f"{k}{t}rf1")
        got(f"{k}{t}rf3")
        share(k, t, 2)

    for k in "ga":
        at(0, first_sends, k)
    at(0.1, lambda: send("basis", grad_basis.at[:, half_of(other)], bg.at[core], sibling))

    def loaded():
        for copy in (own_a, own_g, load_a, load_g):
            copy.wait()
        got("basis")

    at(1.9, loaded)
    for k in "ga":
        at(2, block, k, 0, 0)
        at(4.5, pass_on, k, 0)
        at(6, sides, k, 0)
        at(6.5, partner_block, k, 0)
        at(7.5, both_sides, k, 0)
        at(8, partner_block, k, 1)
        at(8.5, opposite, k, 0)
        at(9.5, block, k, 0, 1)
        at(10.5, pass_on, k, 1)
        at(11, block, k, 2, 0)
        at(12.5, sides, k, 1)
        at(13.5, both_sides, k, 1)
        at(15, opposite, k, 1)
        at(16.5, block, k, 2, 1)
        for t, ready, start in ((0, 10, 12), (1, 14, 16), (3, 14.1, 18), (2, 17, 22)):
            at(ready, spread, k, t)
            at(start + 3, join, k, t)
            at(start + 7, finish, k, t)
            at(start + 11, rounded, k, t)
            at(start + 15, pass_rounded, k, t)
            at(start + 18, opposite_rounded, k, t)
    for _, _, step in sorted(events, key=lambda e: e[:2]):
        step()
    for t in range(4):
        for dr in range(4):
            got(f"g{t}rs{dr}")
    for copy in locals_[4:]:
        copy.wait()
    for copy in copies.values():
        copy.wait_send()


def rotate(acts, grads, act_basis, grad_basis):
    any_space = pl.BlockSpec(memory_space=pl.ANY)
    shape = (4, 2, 4, 2, 32, 512)
    per_chain = lambda *dims, dtype=BF16: [pltpu.VMEM(dims, dtype)] * 2
    return pl.pallas_call(
        exchange_kernel,
        out_shape=(jax.ShapeDtypeStruct(shape, BF16), jax.ShapeDtypeStruct((2,) + shape, BF16)),
        in_specs=[any_space] * 4,
        out_specs=(any_space, any_space),
        scratch_shapes=[
            pltpu.VMEM((4, 2, 2, 128, 1024), BF16),
            pltpu.VMEM((4, 2, 2, 256, 512), BF16),
            pltpu.VMEM((1024, 512), BF16),
            pltpu.VMEM((2, 512, 512), BF16),
            *per_chain(4, 4, 2, 2, 32, 512, dtype=F32),
            *per_chain(4, 4, 2, 2, 32, 512),
            *per_chain(4, 2, 2, 32, 512),
            *per_chain(4, 2, 2, 2, 32, 512),
            *per_chain(4, 2, 2, 32, 512),
            *per_chain(4, 2, 2, 32, 512),
            *per_chain(4, 2, 2, 32, 512),
            pltpu.SemaphoreType.DMA((160,)),
            pltpu.SemaphoreType.DMA((160,)),
            pltpu.SemaphoreType.DMA((16,)),
        ],
        compiler_params=pltpu.CompilerParams(collective_id=0, has_side_effects=True, vmem_limit_bytes=60 << 20),
        cost_estimate=pl.CostEstimate(flops=4 * 2048 * 1024 * 512, bytes_accessed=10 << 20, transcendentals=0),
    )(acts, grads, act_basis, grad_basis)


OUT_ROWS = 512
ALIGN = 16


def tiles_kernel(lengths, order, ra, rg, out):
    out[...] = jnp.zeros_like(out)

    @pl.loop(0, SEQS, init_carry=jnp.int32(0))
    def _(k, start):
        end = start + lengths[order[k]]
        low = start // ALIGN * ALIGN

        def add(rows):
            at = pl.multiple_of(jnp.minimum(low, TOTAL - rows), ALIGN)
            token = at + lax.broadcasted_iota(jnp.int32, (rows, 1), 0)
            a = jnp.where((token >= start) & (token < end), ra[pl.ds(at, rows)], 0)
            tile = lax.dot_general(rg[0, pl.ds(at, rows)], a, (((0,), (0,)), ((), ())), preferred_element_type=F32)
            out[...] += tile * tile

        lax.switch((end - low - 1) // 256, [functools.partial(add, rows) for rows in (256, 512, 768)])
        return end

    out[...] = out[...] * (1.0 / TOTAL)


def tiles(lengths, order, ra, rg):
    smem = pl.BlockSpec(memory_space=pltpu.SMEM)
    per = 512 // OUT_ROWS
    return pl.pallas_call(
        tiles_kernel,
        grid=(1024 // OUT_ROWS,),
        out_shape=jax.ShapeDtypeStruct((1024, 512), F32),
        in_specs=[
            smem,
            smem,
            pl.BlockSpec((TOTAL, 512), lambda i: (0, 0)),
            pl.BlockSpec((1, TOTAL, OUT_ROWS), lambda i: (i // per, 0, i % per)),
        ],
        out_specs=pl.BlockSpec((OUT_ROWS, 512), lambda i: (i, 0)),
        compiler_params=pltpu.CompilerParams(vmem_limit_bytes=60 << 20),
    )(lengths, order, ra, rg)


def shards(activations, gradients, act_basis, grad_basis, lengths, seq_order):
    ra, rg = rotate(activations, gradients, act_basis, grad_basis)
    return tiles(lengths, seq_order, ra.reshape(2048, 512), rg.reshape(2, 2048, 512))


def solution(mesh):
    in_specs = (P("col", "row"), P("row", "col"), P("row", "col"), P("col", "row"), P(), P())
    return jax.shard_map(shards, mesh=mesh, in_specs=in_specs, out_specs=P("row", "col"), check_vma=False)
```

```python
import functools

import jax
import jax.numpy as jnp
from jax import lax
from jax.experimental import pallas as pl
from jax.experimental.pallas import tpu as pltpu
from jax.sharding import PartitionSpec as P

MESH = pl.DeviceIdType.MESH
SEQS = 8
TOTAL = 2048
SCALE = 2.0**28

ACROSS = True
ORDER = (
    "gpair0", "gown0", "basis!", "aown0", "gswap00", "apair0", "gown1", "aswap00", "aown1", "gpair1", "apair1",
    "load", "gdot00", "adot00", "gon10", "aon10", "gring0", "aon30", "gon30", "gswap30", "gswap10", "aswap30",
    "aring0", "aswap10", "gdot30", "gswap01", "gring1", "gdot10", "g1spread", "aswap20", "adot30", "adot10",
    "aring1", "a1spread", "gswap20", "aon11", "gon11", "aswap01", "adot20", "a0spread", "g1join1", "gswap31",
    "g1join3", "gon31", "gswap11", "gdot20", "g0spread", "a1join1", "a1join3", "adot01", "gdot01", "aon31",
    "aswap31", "aswap11", "gdot31", "a0join3", "gdot11", "g2spread", "g0join3", "adot31", "a0join1", "g1finish",
    "adot11", "g0join1", "a2spread", "gswap21", "a1finish", "aswap21", "a0finish", "g2join1", "g2join3", "gdot21",
    "a2join1", "adot21", "g3spread", "a3spread", "a2join3", "g0finish", "g1round", "g2finish", "a1round", "g3join1",
    "g3join3", "a3join3", "a3join1", "a0round", "a2finish", "g0round", "g1share3", "a1pass1", "g1share1", "g1pass1",
    "g1pass3", "g3finish", "a1pass3", "g2round", "a3finish", "a0pass1", "g0share3", "g0share1", "g0pass3",
    "a2round", "a0pass3", "g0pass1", "g1share2", "a1leave", "g3round", "g1leave", "g2share3", "g2share1", "g2pass3",
    "g2pass1", "g0share2", "a3round", "a2pass3", "a2pass1", "a0leave", "g0leave", "g3pass1", "g3pass3", "g3share3",
    "g3share1", "g2share2", "a3pass1", "a3pass3", "g2leave", "g3share2", "a2leave", "g3leave", "a3leave",
)

BF16, F32 = jnp.bfloat16, jnp.float32


def encode(v):
    v = v * SCALE
    return (v * v * v).astype(BF16)


def decode(m):
    v = m.astype(F32)
    size = jnp.abs(v)
    root = jnp.exp2(jnp.log2(jnp.maximum(size, 1e-37)) * (1.0 / 3.0)) * (1.0 / SCALE)
    root = jnp.where(size > 1e-37, root, 0.0)
    return jnp.where(v < 0, -root, root)


def run_tasks(tasks, copies, got):
    for key in ORDER:
        needs, step = tasks.pop(key)
        for name in needs:
            if name in copies:
                got(name)
            else:
                assert name not in tasks
        step()
    assert not tasks


class Place:
    def __init__(self, ring, pair, peer):
        self.ring, self.pair, self.peer = ring, pair, peer

    def to(self, dr=0, dx=0):
        return self.peer(lax.rem(self.ring + dr + 4, 4), lax.rem(self.pair + dx, 2))

    def index(self, dr=0, dx=0):
        return lax.rem(self.ring + dr + 4, 4) * 2 + lax.rem(self.pair + dx, 2)


def exchange_kernel(
    acts, grads, act_basis, grad_basis, out_a, out_g,
    ga, gg, ba, bg, pf_a, pf_g, ms_a, ms_g, ra_a, ra_g, rb_a, rb_g, mx_a, mx_g, rx_a, rx_g, full_a, full_g,
    send_sems, recv_sems, local_sems,
):
    row, col = lax.axis_index("row"), lax.axis_index("col")
    y, xh = row // 2, lax.rem(row, 2)
    z, xl, core = col // 4, lax.rem(col // 2, 2), lax.rem(col, 2)
    other = 1 - core
    along_z = Place(z, xl, lambda r, p: (row, r * 4 + p * 2 + core))
    along_y = Place(y, xh, lambda r, p: (r * 2 + p, col))
    sibling = (row, z * 4 + xl * 2 + other)

    copies, waited, locals_, tasks = {}, set(), [], {}

    def send(name, src, dst, to):
        n = len(copies)
        copy = pltpu.make_async_remote_copy(
            src_ref=src, dst_ref=dst, send_sem=send_sems.at[n], recv_sem=recv_sems.at[n],
            device_id=to, device_id_type=MESH,
        )
        copies[name] = copy
        copy.start()

    def got(name):
        if name not in waited:
            waited.add(name)
            copies[name].wait_recv()

    def local(src, dst):
        copy = pltpu.make_async_copy(src, dst, local_sems.at[len(locals_)])
        locals_.append(copy)
        copy.start()
        return copy

    def task(key, needs, step, *args):
        tasks[key] = (needs, functools.partial(step, *args))

    partners = [along_z.to(1), along_z.to(3), along_z.to(0, 1), along_y.to(1), along_y.to(3), along_y.to(0, 1), sibling]
    barrier = pltpu.get_barrier_semaphore()
    for partner in partners:
        pl.semaphore_signal(barrier, inc=1, device_id=partner, device_id_type=MESH)
    loads = [local(acts, ga.at[0, 0, core]), local(grads, gg.at[0, 0, core]), local(act_basis, ba)]
    half_of = lambda who: pl.ds(pl.multiple_of(who * 512, 512), 512)
    loads.append(local(grad_basis.at[:, half_of(core)], bg.at[core]))
    pl.semaphore_wait(barrier, len(partners))

    chains = {
        "a": dict(mine=acts, g=ga, first=along_z, second=along_y, pf=pf_a, ms=ms_a, ra=ra_a, rb=rb_a, mx=mx_a, rx=rx_a, out=out_a),
        "g": dict(mine=grads, g=gg, first=along_y, second=along_z, pf=pf_g, ms=ms_g, ra=ra_g, rb=rb_g, mx=mx_g, rx=rx_g, out=out_g),
    }

    def loaded():
        for copy in loads:
            copy.wait()

    task("load", ["basis"], loaded)
    task("basis!", [], lambda: send("basis", grad_basis.at[:, half_of(other)], bg.at[core], sibling))

    def half(k, h):
        rows = 64 if k == "a" else 128
        return pl.ds(h * rows, rows)

    def own_ring(k, n):
        c = chains[k]
        mine, g, place = c["mine"], c["g"], c["first"]
        rows = half(k, n)
        send(f"{k}1{n}0", mine.at[rows], g.at[3, 0, core, rows], place.to(1))
        rows = half(k, 1 - n)
        send(f"{k}3{1 - n}0", mine.at[rows], g.at[1, 0, core, rows], place.to(3))

    def own_pair(k, h):
        c = chains[k]
        rows = half(k, h)
        send(f"{k}x{h}", c["mine"].at[rows], c["g"].at[0, 1, core, rows], c["first"].to(0, 1))

    def own_swap(k):
        c = chains[k]
        send(k + "s00", c["mine"], c["g"].at[0, 0, core], sibling)

    def swap(k, dr, dx):
        g = chains[k]["g"]
        send(f"{k}s{dr}{dx}", g.at[dr, dx, core], g.at[dr, dx, core], sibling)

    def pair_ring(k, h):
        g, place = chains[k]["g"], chains[k]["first"]
        rows = half(k, h)
        send(f"{k}1{h}1", g.at[0, 1, core, rows], g.at[3, 1, core, rows], place.to(1))
        send(f"{k}3{h}1", g.at[0, 1, core, rows], g.at[1, 1, core, rows], place.to(3))

    def onward(k, dx, dr, h):
        g, place = chains[k]["g"], chains[k]["first"]
        rows = half(k, h)
        send(f"{k}f{dr}{dx}", g.at[4 - dr, dx, core, rows], g.at[2, dx, core, rows], place.to(dr))

    def spot(k, dr, dx):
        first = chains[k]["first"]
        p, x = lax.rem(first.ring + dr, 4), lax.rem(first.pair + dx, 2)
        return (lax.rem(p, 2) * 2 + x, p // 2) if ACROSS else (p, x)

    def partial(k, dr, dx):
        c = chains[k]
        second, g = c["second"], c["g"]
        p, h = spot(k, dr, dx)

        def keep(value, base):
            for s in range(value.shape[0] // 32):
                o = base + s
                q = lax.rem(o // 2 - second.ring + 4, 4)
                x = lax.rem(o % 2 + second.pair, 2)
                piece = value[s * 32 : (s + 1) * 32]
                c["pf"][q, p, h, x] = piece
                c["ms"][q, p, h, x] = encode(piece)

        for n in range(2):
            if k == "a":
                value = jnp.dot(g[dr, dx, n], ba[...], preferred_element_type=F32)
            else:
                rows = pl.ds(n * 128, 128)
                value = jnp.dot(g[dr, dx, 0, rows], bg[0], preferred_element_type=F32)
                value += jnp.dot(g[dr, dx, 1, rows], bg[1], preferred_element_type=F32)
            keep(value, 4 * n)

    blocks = [[(0, 0), (2, 0)], [(1, 0), (3, 0)], [(1, 1), (3, 1)], [(0, 1), (2, 1)]] if ACROSS else [[(n, 0), (n, 1)] for n in (0, 1, 3, 2)]

    for k in "ga":
        for n in range(2):
            task(f"{k}own{n}", [], own_ring, k, n)
            task(f"{k}pair{n}", [], own_pair, k, n)
            task(f"{k}ring{n}", [f"{k}x{n}"], pair_ring, k, n)
        task(f"{k}swap00", [], own_swap, k)
        task(f"{k}swap01", [f"{k}x0", f"{k}x1"], swap, k, 0, 1)
        arrival = {(0, 0): [], (0, 1): [f"{k}x0", f"{k}x1"]}
        for dx in range(2):
            task(f"{k}on1{dx}", [f"{k}10{dx}"], onward, k, dx, 1, 0)
            task(f"{k}on3{dx}", [f"{k}31{dx}"], onward, k, dx, 3, 1)
            arrival[3, dx] = [f"{k}10{dx}", f"{k}11{dx}"]
            arrival[1, dx] = [f"{k}30{dx}", f"{k}31{dx}"]
            arrival[2, dx] = [f"{k}f1{dx}", f"{k}f3{dx}"]
            for dr in (1, 2, 3):
                task(f"{k}swap{dr}{dx}", arrival[dr, dx], swap, k, dr, dx)
        for (dr, dx), needs in arrival.items():
            task(f"{k}dot{dr}{dx}", ["load", f"{k}s{dr}{dx}"] + needs, partial, k, dr, dx)

    def part_of(k, t):
        return spot(k, *blocks[t][0])[0]

    def spread(k, t):
        c = chains[k]
        ms, ra, rb, place, p = c["ms"], c["ra"], c["rb"], c["second"], part_of(k, t)
        tag = f"{k}{t}"
        send(tag + "a1", ms.at[2, p, 0], ra.at[p, 0], place.to(1))
        send(tag + "a3", ms.at[2, p, 1], ra.at[p, 1], place.to(3))
        send(tag + "b1", ms.at[1, p, 1], rb.at[p, 0, 1], place.to(1))
        send(tag + "b3", ms.at[3, p, 0], rb.at[p, 1, 0], place.to(3))

    def join(k, t, dr, h):
        c = chains[k]
        ms, p = c["ms"], part_of(k, t)
        ms[dr, p, h] = encode(c["pf"][dr, p, h] + decode(c["ra"][p, h]))
        send(f"{k}{t}c{dr}", ms.at[dr, p, h], c["rb"].at[p, h, h], c["second"].to(dr))

    def finish(k, t):
        c = chains[k]
        rb, pf, mx, place, p = c["rb"], c["pf"], c["mx"], c["second"], part_of(k, t)
        total = pf[0, p] + (decode(rb[p, 0]) + decode(rb[p, 1]))
        mx[p] = encode(total)
        send(f"{k}{t}x", mx.at[p], c["rx"].at[p], place.to(0, 1))
        pf[0, p] = total

    def lies(k, t, dr, h=slice(None)):
        p, q = part_of(k, t), lax.rem(chains[k]["second"].ring + dr, 4)
        return (h, p // 2, lax.rem(p, 2), q) if ACROSS else (p // 2, lax.rem(p, 2), h, q)

    def region(k, t, dr, h=slice(None)):
        full = full_a if k == "a" else full_g.at[core]
        return full.at[lies(k, t, dr, h)]

    def rounded(k, t):
        c = chains[k]
        place, p, rx, pf = c["second"], part_of(k, t), c["rx"], c["pf"]
        tag = f"{k}{t}"
        for x in range(2):
            own = lax.rem(place.pair + x, 2)
            for h in range(2):
                value = (pf[0, p, h, x] + decode(rx[p, h, 1 - x])).astype(BF16)
                if k == "a":
                    full_a[lies(k, t, 0, h) + (own,)] = value
                else:
                    full_g[(core,) + lies(k, t, 0, h) + (own,)] = value
        mine = region(k, t, 0)
        send(tag + "r1", mine, mine, place.to(1))
        send(tag + "r3", mine, mine, place.to(3))
        if k == "g":
            send(tag + "s0", mine, mine, sibling)

    def share(k, t, dr):
        send(f"{k}{t}s{dr}", region(k, t, dr), region(k, t, dr), sibling)

    def pass_rounded(k, t, dr, h):
        there = region(k, t, 4 - dr, h)
        send(f"{k}{t}f{dr}", there, there, chains[k]["second"].to(dr))

    def leave(k, t):
        p = part_of(k, t)
        at = (slice(None), p // 2, lax.rem(p, 2)) if ACROSS else (p // 2, lax.rem(p, 2))
        if k == "a":
            local(full_a.at[at], out_a.at[at])
        else:
            for n in range(2):
                local(full_g.at[(n,) + at], out_g.at[(n,) + at])

    for k in "ga":
        for t in range(4):
            tag = f"{k}{t}"
            task(tag + "spread", [f"{k}dot{dr}{dx}" for dr, dx in blocks[t]], spread, k, t)
            task(tag + "join1", [tag + "a1"], join, k, t, 1, 0)
            task(tag + "join3", [tag + "a3"], join, k, t, 3, 1)
            task(tag + "finish", [tag + n for n in ("b1", "b3", "c1", "c3")], finish, k, t)
            task(tag + "round", [tag + "x"], rounded, k, t)
            task(tag + "pass1", [tag + "r1"], pass_rounded, k, t, 1, 0)
            task(tag + "pass3", [tag + "r3"], pass_rounded, k, t, 3, 1)
            if k == "g":
                task(tag + "share3", [tag + "r1"], share, k, t, 3)
                task(tag + "share1", [tag + "r3"], share, k, t, 1)
                task(tag + "share2", [tag + "f1", tag + "f3"], share, k, t, 2)
            shared = [f"{tag}s{dr}" for dr in range(4)] if k == "g" else []
            task(tag + "leave", [tag + "round", tag + "r1", tag + "r3", tag + "f1", tag + "f3"] + shared, leave, k, t)

    run_tasks(tasks, copies, got)
    for name in copies:
        got(name)
    for copy in locals_[len(loads):]:
        copy.wait()
    for copy in copies.values():
        copy.wait_send()


def rotate(acts, grads, act_basis, grad_basis):
    any_space = pl.BlockSpec(memory_space=pl.ANY)
    shape = (2, 2, 2, 4, 2, 32, 512)
    per_chain = lambda *dims, dtype=BF16: [pltpu.VMEM(dims, dtype)] * 2
    return pl.pallas_call(
        exchange_kernel,
        out_shape=(jax.ShapeDtypeStruct(shape, BF16), jax.ShapeDtypeStruct((2,) + shape, BF16)),
        in_specs=[any_space] * 4,
        out_specs=(any_space, any_space),
        scratch_shapes=[
            pltpu.VMEM((4, 2, 2, 128, 1024), BF16),
            pltpu.VMEM((4, 2, 2, 256, 512), BF16),
            pltpu.VMEM((1024, 512), BF16),
            pltpu.VMEM((2, 512, 512), BF16),
            *per_chain(4, 4, 2, 2, 32, 512, dtype=F32),
            *per_chain(4, 4, 2, 2, 32, 512),
            *per_chain(4, 2, 2, 32, 512),
            *per_chain(4, 2, 2, 2, 32, 512),
            *per_chain(4, 2, 2, 32, 512),
            *per_chain(4, 2, 2, 32, 512),
            pltpu.VMEM(shape, BF16),
            pltpu.VMEM((2,) + shape, BF16),
            pltpu.SemaphoreType.DMA((160,)),
            pltpu.SemaphoreType.DMA((160,)),
            pltpu.SemaphoreType.DMA((16,)),
        ],
        compiler_params=pltpu.CompilerParams(collective_id=0, has_side_effects=True, vmem_limit_bytes=60 << 20),
        cost_estimate=pl.CostEstimate(flops=4 * 2048 * 1024 * 512, bytes_accessed=10 << 20, transcendentals=0),
    )(acts, grads, act_basis, grad_basis)


ALIGN = 16
CHUNK = 512


def tiles_kernel(lengths, order, ra_hbm, rg_hbm, out, ra, rg, sems):
    def chunk(n):
        rows = pl.ds(pl.multiple_of(n * CHUNK, CHUNK), CHUNK)
        return [pltpu.make_async_copy(ra_hbm.at[rows], ra.at[rows], sems.at[n, 0])] + [
            pltpu.make_async_copy(rg_hbm.at[h, rows], rg.at[rows, pl.ds(h * 512, 512)], sems.at[n, 1 + h])
            for h in range(2)
        ]

    for n in range(TOTAL // CHUNK):
        for copy in chunk(n):
            copy.start()
    out[...] = jnp.zeros_like(out)

    @pl.loop(0, SEQS, init_carry=(jnp.int32(0), jnp.int32(0)))
    def _(k, carry):
        start, here = carry
        end = start + lengths[order[k]]
        low = start // ALIGN * ALIGN
        size = (end - low + 255) // 256 * 256
        low = jnp.minimum(low, TOTAL - size)
        needed = (low + size + CHUNK - 1) // CHUNK

        @pl.loop(here, needed)
        def _(n):
            for copy in chunk(n):
                copy.wait()

        def add(rows):
            at = pl.multiple_of(low, ALIGN)
            token = at + lax.broadcasted_iota(jnp.int32, (rows, 1), 0)
            a = jnp.where((token >= start) & (token < end), ra[pl.ds(at, rows)], 0)
            tile = lax.dot_general(rg[pl.ds(at, rows)], a, (((0,), (0,)), ((), ())), preferred_element_type=F32)
            out[...] += tile * (tile * (1.0 / TOTAL))

        lax.switch(size // 256 - 1, [functools.partial(add, rows) for rows in (256, 512, 768)])
        return end, jnp.maximum(here, needed)


def tiles(lengths, order, ra, rg):
    smem, anywhere = pl.BlockSpec(memory_space=pltpu.SMEM), pl.BlockSpec(memory_space=pl.ANY)
    return pl.pallas_call(
        tiles_kernel,
        out_shape=jax.ShapeDtypeStruct((1024, 512), F32),
        in_specs=[smem, smem, anywhere, anywhere],
        out_specs=pl.BlockSpec(memory_space=pltpu.VMEM),
        scratch_shapes=[
            pltpu.VMEM((TOTAL, 512), BF16),
            pltpu.VMEM((TOTAL, 1024), BF16),
            pltpu.SemaphoreType.DMA((TOTAL // CHUNK, 3)),
        ],
        compiler_params=pltpu.CompilerParams(vmem_limit_bytes=60 << 20),
    )(lengths, order, ra, rg)


def shards(activations, gradients, act_basis, grad_basis, lengths, seq_order):
    ra, rg = rotate(activations, gradients, act_basis, grad_basis)
    return tiles(lengths, seq_order, ra.reshape(2048, 512), rg.reshape(2, 2048, 512))


def solution(mesh):
    in_specs = (P("col", "row"), P("row", "col"), P("row", "col"), P("col", "row"), P(), P())
    return jax.shard_map(shards, mesh=mesh, in_specs=in_specs, out_specs=P("row", "col"), check_vma=False)
```

```python
import functools

import jax
import jax.numpy as jnp
from jax import lax
from jax.experimental import pallas as pl
from jax.experimental.pallas import tpu as pltpu
from jax.sharding import PartitionSpec as P

MESH = pl.DeviceIdType.MESH
SEQS = 8
TOTAL = 2048
SCALE = 2.0**28

PIECES = 4
VIA_PAIR = {"a": (0, 1, 2, 3), "g": (0, 1, 2, 3)}
IN_FLIGHT = 60
FAR_SUM = ()
FAR_OUT = ()
ORDER = (
    7, 43, 13, 49, 39, 3, 8, 44, 18, 54, 12, 48, 2, 38, 53, 17, 22, 58, 0, 10, 15, 46, 51, 14, 1, 23, 50, 74, 59,
    56, 41, 20, 5, 154, 40, 34, 70, 62, 26, 4, 11, 16, 52, 47, 9, 35, 134, 45, 71, 6, 21, 30, 75, 190, 63, 19, 27,
    57, 42, 155, 66, 24, 94, 55, 60, 166, 31, 114, 135, 67, 178, 25, 84, 191, 61, 160, 36, 28, 76, 156, 95, 64, 37,
    144, 167, 115, 32, 72, 179, 29, 192, 136, 104, 65, 172, 85, 161, 68, 33, 124, 96, 73, 196, 77, 168, 79, 145,
    180, 157, 116, 69, 184, 105, 173, 193, 86, 137, 162, 125, 139, 197, 97, 99, 81, 78, 80, 169, 158, 146, 106, 185,
    181, 138, 141, 194, 140, 117, 119, 174, 126, 198, 87, 98, 89, 100, 101, 82, 163, 170, 186, 147, 142, 149, 159,
    83, 121, 182, 107, 118, 120, 109, 88, 90, 143, 195, 175, 91, 164, 102, 127, 129, 148, 150, 151, 171, 199, 183,
    103, 111, 108, 110, 187, 176, 92, 122, 165, 128, 131, 130, 93, 123, 200, 152, 112, 188, 153, 177, 113, 132, 201,
    133, 189,
)

BF16, F32 = jnp.bfloat16, jnp.float32


def encode(v):
    v = v * SCALE
    return (v * v * v).astype(BF16)


def decode(m):
    v = m.astype(F32)
    size = jnp.abs(v)
    root = jnp.exp2(jnp.log2(jnp.maximum(size, 1e-37)) * (1.0 / 3.0)) * (1.0 / SCALE)
    root = jnp.where(size > 1e-37, root, 0.0)
    return jnp.where(v < 0, -root, root)


def run_tasks(tasks, copies, got):
    steps, done = list(tasks.items()), set()
    for n in ORDER:
        key, (needs, step) = steps[n]
        for name in needs:
            if name in copies:
                got(name)
            else:
                assert name in done
        step()
        done.add(key)
    assert len(done) == len(steps)


class Place:
    def __init__(self, ring, pair, peer):
        self.ring, self.pair, self.peer = ring, pair, peer

    def to(self, dr=0, dx=0):
        return self.peer(lax.rem(self.ring + dr + 4, 4), lax.rem(self.pair + dx, 2))

    def index(self, dr=0, dx=0):
        return lax.rem(self.ring + dr + 4, 4) * 2 + lax.rem(self.pair + dx, 2)


def exchange_kernel(
    acts, grads, act_basis, grad_basis, out_a, out_g,
    ga, gg, ba, bg, pf_a, pf_g, ms_a, ms_g, ra_a, ra_g, rb_a, rb_g, mx_a, mx_g, rx_a, rx_g, full_a, full_g,
    send_sems, recv_sems, local_sems,
):
    row, col = lax.axis_index("row"), lax.axis_index("col")
    y, xh = row // 2, lax.rem(row, 2)
    z, xl, core = col // 4, lax.rem(col // 2, 2), lax.rem(col, 2)
    other = 1 - core
    along_z = Place(z, xl, lambda r, p: (row, r * 4 + p * 2 + core))
    along_y = Place(y, xh, lambda r, p: (r * 2 + p, col))
    sibling = (row, z * 4 + xl * 2 + other)

    copies, waited, sent, locals_, tasks = {}, set(), [], [], {}

    def send(name, src, dst, to):
        n = len(copies)
        copy = pltpu.make_async_remote_copy(
            src_ref=src, dst_ref=dst, send_sem=send_sems.at[n], recv_sem=recv_sems.at[n],
            device_id=to, device_id_type=MESH,
        )
        copies[name] = copy
        copy.start()
        sent.append(copy)
        if len(sent) > IN_FLIGHT:
            sent.pop(0).wait_send()

    def got(name):
        if name not in waited:
            waited.add(name)
            copies[name].wait_recv()

    def local(src, dst):
        copy = pltpu.make_async_copy(src, dst, local_sems.at[len(locals_)])
        locals_.append(copy)
        copy.start()
        return copy

    def task(key, needs, step, *args):
        tasks[key] = (needs, functools.partial(step, *args))

    partners = [along_z.to(1), along_z.to(3), along_z.to(0, 1), along_y.to(1), along_y.to(3), along_y.to(0, 1), sibling]
    if FAR_SUM or FAR_OUT:
        partners += [along_z.to(2), along_y.to(2)]
    barrier = pltpu.get_barrier_semaphore()
    for partner in partners:
        pl.semaphore_signal(barrier, inc=1, device_id=partner, device_id_type=MESH)
    loads = [local(acts, ga.at[0, 0, core]), local(grads, gg.at[0, 0, core]), local(act_basis, ba)]
    half_of = lambda who: pl.ds(pl.multiple_of(who * 512, 512), 512)
    loads.append(local(grad_basis.at[:, half_of(core)], bg.at[core]))
    pl.semaphore_wait(barrier, len(partners))

    chains = {
        "a": dict(mine=acts, g=ga, first=along_z, second=along_y, pf=pf_a, ms=ms_a, ra=ra_a, rb=rb_a, mx=mx_a, rx=rx_a),
        "g": dict(mine=grads, g=gg, first=along_y, second=along_z, pf=pf_g, ms=ms_g, ra=ra_g, rb=rb_g, mx=mx_g, rx=rx_g),
    }

    def loaded():
        for copy in loads:
            copy.wait()

    def basis():
        send("basis", grad_basis.at[:, half_of(other)], bg.at[core], sibling)

    task("swap", [], basis)
    task("load", ["basis"], loaded)

    def piece(k, n):
        rows = (128 if k == "a" else 256) // PIECES
        return pl.ds(n * rows, rows)

    def own_ring(k, n):
        c = chains[k]
        mine, g, place = c["mine"], c["g"], c["first"]
        rows = piece(k, n)
        send((k, "in", 3, 0, n), mine.at[rows], g.at[3, 0, core, rows], place.to(1))
        n = PIECES - 1 - n
        rows = piece(k, n)
        send((k, "in", 1, 0, n), mine.at[rows], g.at[1, 0, core, rows], place.to(3))

    def own_pair(k, n):
        c = chains[k]
        rows = piece(k, n)
        send((k, "in", 0, 1, n), c["mine"].at[rows], c["g"].at[0, 1, core, rows], c["first"].to(0, 1))

    def own_swap(k):
        c = chains[k]
        send((k, "swap", 0, 0), c["mine"], c["g"].at[0, 0, core], sibling)

    def swap(k, dr, dx):
        g = chains[k]["g"]
        send((k, "swap", dr, dx), g.at[dr, dx, core], g.at[dr, dx, core], sibling)

    def pair_ring(k, n):
        g, place = chains[k]["g"], chains[k]["first"]
        rows = piece(k, n)
        send((k, "in", 3, 1, n), g.at[0, 1, core, rows], g.at[3, 1, core, rows], place.to(1))
        send((k, "in", 1, 1, n), g.at[0, 1, core, rows], g.at[1, 1, core, rows], place.to(3))

    def onward(k, dx, n):
        g, place = chains[k]["g"], chains[k]["first"]
        rows = piece(k, n)
        if dx == 1 and n in VIA_PAIR[k]:
            send((k, "in", 2, 1, n), g.at[2, 0, core, rows], g.at[2, 1, core, rows], place.to(0, 1))
            return
        dr = 1 if n < PIECES // 2 else 3
        send((k, "in", 2, dx, n), g.at[4 - dr, dx, core, rows], g.at[2, dx, core, rows], place.to(dr))

    def spot(k, dr, dx):
        first = chains[k]["first"]
        return lax.rem(first.ring + dr, 4), lax.rem(first.pair + dx, 2)

    def partial(k, dr, dx):
        c = chains[k]
        second, g = c["second"], c["g"]
        p, i = spot(k, dr, dx)

        def keep(value, base):
            for s in range(value.shape[0] // 32):
                o = base + s
                q = lax.rem(o // 2 - second.ring + 4, 4)
                x = lax.rem(o % 2 + second.pair, 2)
                piece = value[s * 32 : (s + 1) * 32]
                c["pf"][q, p, i, x] = piece
                c["ms"][q, p, i, x] = encode(piece)

        for n in range(2):
            if k == "a":
                value = jnp.dot(g[dr, dx, n], ba[...], preferred_element_type=F32)
            else:
                rows = pl.ds(n * 128, 128)
                value = jnp.dot(g[dr, dx, 0, rows], bg[0], preferred_element_type=F32)
                value += jnp.dot(g[dr, dx, 1, rows], bg[1], preferred_element_type=F32)
            keep(value, 4 * n)

    for k in "ga":
        for n in range(PIECES):
            task((k, "own", n), [], own_ring, k, n)
            task((k, "pair", n), [], own_pair, k, n)
            task((k, "ring", n), [(k, "in", 0, 1, n)], pair_ring, k, n)
            for dx in range(2):
                needs = [(k, "in", 3 if n < PIECES // 2 else 1, dx, n)]
                if dx == 1 and n in VIA_PAIR[k]:
                    needs = [(k, "in", 2, 0, n)]
                task((k, "on", n, dx), needs, onward, k, dx, n)
        task((k, "swap", 0, 0, "!"), [], own_swap, k)
        for dr in range(4):
            for dx in range(2):
                needs = [(k, "in", dr, dx, n) for n in range(PIECES)] if dr + dx else []
                if needs:
                    task((k, "swap", dr, dx, "!"), needs, swap, k, dr, dx)
                task((k, "dot", dr, dx), ["load", (k, "swap", dr, dx)] + needs, partial, k, dr, dx)

    def ways(p):
        h = p // 2
        return h, 1 + 2 * h, 3 - 2 * h

    def spread(k, dr, dx):
        c = chains[k]
        p, i = spot(k, dr, dx)
        h, way, back = ways(p)
        far = (dr, dx) in FAR_SUM
        if far:
            send((k, "c", dr, dx), c["ms"].at[way, p, i], c["rb"].at[h, p, i], c["second"].to(way))
        send((k, "a", dr, dx), c["ms"].at[2, p, i], c["ra"].at[p, i], c["second"].to(2 if far else way))
        send((k, "b", dr, dx), c["ms"].at[back, p, i], c["rb"].at[1 - h, p, i], c["second"].to(back))

    def join(k, dr, dx):
        c = chains[k]
        p, i = spot(k, dr, dx)
        h, way, _ = ways(p)
        c["ms"][way, p, i] = encode(c["pf"][way, p, i] + decode(c["ra"][p, i]))
        send((k, "c", dr, dx), c["ms"].at[way, p, i], c["rb"].at[h, p, i], c["second"].to(way))

    def finish(k, dr, dx):
        c = chains[k]
        p, i = spot(k, dr, dx)
        total = c["pf"][0, p, i] + (decode(c["rb"][0, p, i]) + decode(c["rb"][1, p, i]))
        if (dr, dx) in FAR_SUM:
            total += decode(c["ra"][p, i])
        c["mx"][p, i] = encode(total)
        send((k, "x", dr, dx), c["mx"].at[p, i], c["rx"].at[p, i], c["second"].to(0, 1))
        c["pf"][0, p, i] = total

    def region(k, dr, dx, away):
        p, i = spot(k, dr, dx)
        full = full_a if k == "a" else full_g.at[core]
        return full.at[p, i, lax.rem(chains[k]["second"].ring + away, 4)]

    def rounded(k, dr, dx):
        c = chains[k]
        place = c["second"]
        p, i = spot(k, dr, dx)
        _, way, back = ways(p)
        for x in range(2):
            own = lax.rem(place.pair + x, 2)
            value = (c["pf"][0, p, i, x] + decode(c["rx"][p, i, 1 - x])).astype(BF16)
            if k == "a":
                full_a[p, i, place.ring, own] = value
            else:
                full_g[core, p, i, place.ring, own] = value
        mine = region(k, dr, dx, 0)
        send((k, "r", dr, dx), mine, mine, place.to(way))
        send((k, "s", dr, dx), mine, mine, place.to(back))
        if (dr, dx) in FAR_OUT:
            send((k, "f", dr, dx), mine, mine, place.to(2))

    def onward_rounded(k, dr, dx):
        _, way, back = ways(spot(k, dr, dx)[0])
        there = region(k, dr, dx, back)
        send((k, "f", dr, dx), there, there, chains[k]["second"].to(way))

    def share(dr, dx, n):
        _, way, back = ways(spot("g", dr, dx)[0])
        there = region("g", dr, dx, (0, back, way, 2)[n])
        send(("t", n, dr, dx), there, there, sibling)

    def leave(k, dr, dx):
        p, i = spot(k, dr, dx)
        if k == "a":
            local(full_a.at[p, i], out_a.at[p, i])
        else:
            for n in range(2):
                local(full_g.at[n, p, i], out_g.at[n, p, i])

    for k in "ga":
        for dr in range(4):
            for dx in range(2):
                at = (dr, dx)
                task((k, "spread") + at, [(k, "dot") + at], spread, k, dr, dx)
                sums = [(k, "b") + at, (k, "c") + at]
                if at in FAR_SUM:
                    sums.append((k, "a") + at)
                else:
                    task((k, "join") + at, [(k, "a") + at], join, k, dr, dx)
                task((k, "end") + at, sums, finish, k, dr, dx)
                task((k, "round") + at, [(k, "x") + at], rounded, k, dr, dx)
                if at not in FAR_OUT:
                    task((k, "pass") + at, [(k, "r") + at], onward_rounded, k, dr, dx)
                arrivals = [(k, "r") + at, (k, "s") + at, (k, "f") + at]
                needs = [(k, "round") + at] + arrivals
                if k == "g":
                    for n in range(4):
                        task(("share", n) + at, [needs[n]], share, dr, dx, n)
                        needs.append(("t", n) + at)
                task((k, "leave") + at, needs, leave, k, dr, dx)

    run_tasks(tasks, copies, got)
    for copy in locals_[len(loads):]:
        copy.wait()
    for copy in sent:
        copy.wait_send()


def rotate(acts, grads, act_basis, grad_basis):
    any_space = pl.BlockSpec(memory_space=pl.ANY)
    shape = (4, 2, 4, 2, 32, 512)
    per_chain = lambda *dims, dtype=BF16: [pltpu.VMEM(dims, dtype)] * 2
    return pl.pallas_call(
        exchange_kernel,
        out_shape=(jax.ShapeDtypeStruct(shape, BF16), jax.ShapeDtypeStruct((2,) + shape, BF16)),
        in_specs=[any_space] * 4,
        out_specs=(any_space, any_space),
        scratch_shapes=[
            pltpu.VMEM((4, 2, 2, 128, 1024), BF16),
            pltpu.VMEM((4, 2, 2, 256, 512), BF16),
            pltpu.VMEM((1024, 512), BF16),
            pltpu.VMEM((2, 512, 512), BF16),
            *per_chain(4, 4, 2, 2, 32, 512, dtype=F32),
            *per_chain(4, 4, 2, 2, 32, 512),
            *per_chain(4, 2, 2, 32, 512),
            *per_chain(2, 4, 2, 2, 32, 512),
            *per_chain(4, 2, 2, 32, 512),
            *per_chain(4, 2, 2, 32, 512),
            pltpu.VMEM(shape, BF16),
            pltpu.VMEM((2,) + shape, BF16),
            pltpu.SemaphoreType.DMA((260,)),
            pltpu.SemaphoreType.DMA((260,)),
            pltpu.SemaphoreType.DMA((32,)),
        ],
        compiler_params=pltpu.CompilerParams(collective_id=0, has_side_effects=True, vmem_limit_bytes=60 << 20),
        cost_estimate=pl.CostEstimate(flops=4 * 2048 * 1024 * 512, bytes_accessed=10 << 20, transcendentals=0),
    )(acts, grads, act_basis, grad_basis)


ALIGN = 16
CHUNK = 512


def tiles_kernel(lengths, order, ra_hbm, rg_hbm, out, ra, rg, sems):
    def chunk(n):
        rows = pl.ds(pl.multiple_of(n * CHUNK, CHUNK), CHUNK)
        return [pltpu.make_async_copy(ra_hbm.at[rows], ra.at[rows], sems.at[n, 0])] + [
            pltpu.make_async_copy(rg_hbm.at[h, rows], rg.at[rows, pl.ds(h * 512, 512)], sems.at[n, 1 + h])
            for h in range(2)
        ]

    for n in range(TOTAL // CHUNK):
        for copy in chunk(n):
            copy.start()
    out[...] = jnp.zeros_like(out)

    @pl.loop(0, SEQS, init_carry=(jnp.int32(0), jnp.int32(0)))
    def _(k, carry):
        start, here = carry
        end = start + lengths[order[k]]
        low = start // ALIGN * ALIGN
        size = (end - low + 255) // 256 * 256
        low = jnp.minimum(low, TOTAL - size)
        needed = (low + size + CHUNK - 1) // CHUNK

        @pl.loop(here, needed)
        def _(n):
            for copy in chunk(n):
                copy.wait()

        def add(rows):
            at = pl.multiple_of(low, ALIGN)
            token = at + lax.broadcasted_iota(jnp.int32, (rows, 1), 0)
            a = jnp.where((token >= start) & (token < end), ra[pl.ds(at, rows)], 0)
            tile = lax.dot_general(rg[pl.ds(at, rows)], a, (((0,), (0,)), ((), ())), preferred_element_type=F32)
            out[...] += tile * (tile * (1.0 / TOTAL))

        lax.switch(size // 256 - 1, [functools.partial(add, rows) for rows in (256, 512, 768)])
        return end, jnp.maximum(here, needed)


def tiles(lengths, order, ra, rg):
    smem, anywhere = pl.BlockSpec(memory_space=pltpu.SMEM), pl.BlockSpec(memory_space=pl.ANY)
    return pl.pallas_call(
        tiles_kernel,
        out_shape=jax.ShapeDtypeStruct((1024, 512), F32),
        in_specs=[smem, smem, anywhere, anywhere],
        out_specs=pl.BlockSpec(memory_space=pltpu.VMEM),
        scratch_shapes=[
            pltpu.VMEM((TOTAL, 512), BF16),
            pltpu.VMEM((TOTAL, 1024), BF16),
            pltpu.SemaphoreType.DMA((TOTAL // CHUNK, 3)),
        ],
        compiler_params=pltpu.CompilerParams(vmem_limit_bytes=60 << 20),
    )(lengths, order, ra, rg)


def shards(activations, gradients, act_basis, grad_basis, lengths, seq_order):
    ra, rg = rotate(activations, gradients, act_basis, grad_basis)
    return tiles(lengths, seq_order, ra.reshape(2048, 512), rg.reshape(2, 2048, 512))


def solution(mesh):
    in_specs = (P("col", "row"), P("row", "col"), P("row", "col"), P("col", "row"), P(), P())
    return jax.shard_map(shards, mesh=mesh, in_specs=in_specs, out_specs=P("row", "col"), check_vma=False)
```

```python
import functools

import jax
import jax.numpy as jnp
from jax import lax
from jax.experimental import pallas as pl
from jax.experimental.pallas import tpu as pltpu
from jax.sharding import PartitionSpec as P

MESH = pl.DeviceIdType.MESH
SEQS = 8
TOTAL = 2048
SCALE = 2.0**40
TINY = 2.0**-126

PIECES = 4
VIA_PAIR = {"a": (0, 1, 2, 3), "g": (0, 1, 2, 3)}
IN_FLIGHT = 60
FAR_SUM = ()
FAR_OUT = ()
ORDER = (
    7, 43, 13, 49, 39, 3, 8, 44, 18, 54, 12, 48, 2, 38, 53, 17, 22, 58, 0, 10, 15, 46, 51, 14, 1, 23, 50, 74, 59,
    56, 41, 20, 5, 154, 40, 34, 70, 62, 26, 4, 11, 16, 52, 47, 9, 35, 134, 45, 71, 6, 21, 30, 75, 190, 63, 19, 27,
    57, 42, 155, 66, 24, 94, 55, 60, 166, 31, 114, 135, 67, 178, 25, 84, 191, 61, 160, 36, 28, 76, 156, 95, 64, 37,
    144, 167, 115, 32, 72, 179, 29, 192, 136, 104, 65, 172, 85, 161, 68, 33, 124, 96, 73, 196, 77, 168, 79, 145,
    180, 157, 116, 69, 184, 105, 173, 193, 86, 137, 162, 125, 139, 197, 97, 99, 81, 78, 80, 169, 158, 146, 106, 185,
    181, 138, 141, 194, 140, 117, 119, 174, 126, 198, 87, 98, 89, 100, 101, 82, 163, 170, 186, 147, 142, 149, 159,
    83, 121, 182, 107, 118, 120, 109, 88, 90, 143, 195, 175, 91, 164, 102, 127, 129, 148, 150, 151, 171, 199, 183,
    103, 111, 108, 110, 187, 176, 92, 122, 165, 128, 131, 130, 93, 123, 200, 152, 112, 188, 153, 177, 113, 132, 201,
    133, 189,
)

BF16, F32 = jnp.bfloat16, jnp.float32


def encode(v):
    v = v * SCALE
    size = jnp.abs(v)
    return (v * (size * jnp.sqrt(size))).astype(BF16)


def decode(m):
    v = m.astype(F32)
    size = jnp.abs(v)
    root = jnp.exp2(jnp.log2(jnp.maximum(size, TINY)) * 0.4) * (1.0 / SCALE)
    root = jnp.where(size >= TINY, root, 0.0)
    return jnp.where(v < 0, -root, root)


def run_tasks(tasks, copies, got):
    steps, done = list(tasks.items()), set()
    for n in ORDER:
        key, (needs, step) = steps[n]
        for name in needs:
            if name in copies:
                got(name)
            else:
                assert name in done
        step()
        done.add(key)
    assert len(done) == len(steps)


class Place:
    def __init__(self, ring, pair, peer):
        self.ring, self.pair, self.peer = ring, pair, peer

    def to(self, dr=0, dx=0):
        return self.peer(lax.rem(self.ring + dr + 4, 4), lax.rem(self.pair + dx, 2))

    def index(self, dr=0, dx=0):
        return lax.rem(self.ring + dr + 4, 4) * 2 + lax.rem(self.pair + dx, 2)


def exchange_kernel(
    acts, grads, act_basis, grad_basis, out_a, out_g,
    ga, gg, ba, bg, pf_a, pf_g, ms_a, ms_g, ra_a, ra_g, rb_a, rb_g, mx_a, mx_g, rx_a, rx_g, full_a, full_g,
    send_sems, recv_sems, local_sems,
):
    row, col = lax.axis_index("row"), lax.axis_index("col")
    y, xh = row // 2, lax.rem(row, 2)
    z, xl, core = col // 4, lax.rem(col // 2, 2), lax.rem(col, 2)
    other = 1 - core
    along_z = Place(z, xl, lambda r, p: (row, r * 4 + p * 2 + core))
    along_y = Place(y, xh, lambda r, p: (r * 2 + p, col))
    sibling = (row, z * 4 + xl * 2 + other)

    copies, waited, sent, locals_, tasks = {}, set(), [], [], {}

    def send(name, src, dst, to):
        n = len(copies)
        copy = pltpu.make_async_remote_copy(
            src_ref=src, dst_ref=dst, send_sem=send_sems.at[n], recv_sem=recv_sems.at[n],
            device_id=to, device_id_type=MESH,
        )
        copies[name] = copy
        copy.start()
        sent.append(copy)
        if len(sent) > IN_FLIGHT:
            sent.pop(0).wait_send()

    def got(name):
        if name not in waited:
            waited.add(name)
            copies[name].wait_recv()

    def local(src, dst):
        copy = pltpu.make_async_copy(src, dst, local_sems.at[len(locals_)])
        locals_.append(copy)
        copy.start()
        return copy

    def task(key, needs, step, *args):
        tasks[key] = (needs, functools.partial(step, *args))

    partners = [along_z.to(1), along_z.to(3), along_z.to(0, 1), along_y.to(1), along_y.to(3), along_y.to(0, 1), sibling]
    if FAR_SUM or FAR_OUT:
        partners += [along_z.to(2), along_y.to(2)]
    barrier = pltpu.get_barrier_semaphore()
    for partner in partners:
        pl.semaphore_signal(barrier, inc=1, device_id=partner, device_id_type=MESH)
    loads = [local(acts, ga.at[0, 0, core]), local(grads, gg.at[0, 0, core]), local(act_basis, ba)]
    half_of = lambda who: pl.ds(pl.multiple_of(who * 512, 512), 512)
    loads.append(local(grad_basis.at[:, half_of(core)], bg.at[core]))
    pl.semaphore_wait(barrier, len(partners))

    chains = {
        "a": dict(mine=acts, g=ga, first=along_z, second=along_y, pf=pf_a, ms=ms_a, ra=ra_a, rb=rb_a, mx=mx_a, rx=rx_a),
        "g": dict(mine=grads, g=gg, first=along_y, second=along_z, pf=pf_g, ms=ms_g, ra=ra_g, rb=rb_g, mx=mx_g, rx=rx_g),
    }

    def loaded():
        for copy in loads:
            copy.wait()

    def basis():
        send("basis", grad_basis.at[:, half_of(other)], bg.at[core], sibling)

    task("swap", [], basis)
    task("load", ["basis"], loaded)

    def piece(k, n):
        rows = (128 if k == "a" else 256) // PIECES
        return pl.ds(n * rows, rows)

    def own_ring(k, n):
        c = chains[k]
        mine, g, place = c["mine"], c["g"], c["first"]
        rows = piece(k, n)
        send((k, "in", 3, 0, n), mine.at[rows], g.at[3, 0, core, rows], place.to(1))
        n = PIECES - 1 - n
        rows = piece(k, n)
        send((k, "in", 1, 0, n), mine.at[rows], g.at[1, 0, core, rows], place.to(3))

    def own_pair(k, n):
        c = chains[k]
        rows = piece(k, n)
        send((k, "in", 0, 1, n), c["mine"].at[rows], c["g"].at[0, 1, core, rows], c["first"].to(0, 1))

    def own_swap(k):
        c = chains[k]
        send((k, "swap", 0, 0), c["mine"], c["g"].at[0, 0, core], sibling)

    def swap(k, dr, dx):
        g = chains[k]["g"]
        send((k, "swap", dr, dx), g.at[dr, dx, core], g.at[dr, dx, core], sibling)

    def pair_ring(k, n):
        g, place = chains[k]["g"], chains[k]["first"]
        rows = piece(k, n)
        send((k, "in", 3, 1, n), g.at[0, 1, core, rows], g.at[3, 1, core, rows], place.to(1))
        send((k, "in", 1, 1, n), g.at[0, 1, core, rows], g.at[1, 1, core, rows], place.to(3))

    def onward(k, dx, n):
        g, place = chains[k]["g"], chains[k]["first"]
        rows = piece(k, n)
        if dx == 1 and n in VIA_PAIR[k]:
            send((k, "in", 2, 1, n), g.at[2, 0, core, rows], g.at[2, 1, core, rows], place.to(0, 1))
            return
        dr = 1 if n < PIECES // 2 else 3
        send((k, "in", 2, dx, n), g.at[4 - dr, dx, core, rows], g.at[2, dx, core, rows], place.to(dr))

    def spot(k, dr, dx):
        first = chains[k]["first"]
        return lax.rem(first.ring + dr, 4), lax.rem(first.pair + dx, 2)

    def partial(k, dr, dx):
        c = chains[k]
        second, g = c["second"], c["g"]
        p, i = spot(k, dr, dx)

        def keep(value, base):
            for s in range(value.shape[0] // 32):
                o = base + s
                q = lax.rem(o // 2 - second.ring + 4, 4)
                x = lax.rem(o % 2 + second.pair, 2)
                piece = value[s * 32 : (s + 1) * 32]
                c["pf"][q, p, i, x] = piece
                c["ms"][q, p, i, x] = encode(piece)

        for n in range(2):
            if k == "a":
                value = jnp.dot(g[dr, dx, n], ba[...], preferred_element_type=F32)
            else:
                rows = pl.ds(n * 128, 128)
                value = jnp.dot(g[dr, dx, 0, rows], bg[0], preferred_element_type=F32)
                value += jnp.dot(g[dr, dx, 1, rows], bg[1], preferred_element_type=F32)
            keep(value, 4 * n)

    for k in "ga":
        for n in range(PIECES):
            task((k, "own", n), [], own_ring, k, n)
            task((k, "pair", n), [], own_pair, k, n)
            task((k, "ring", n), [(k, "in", 0, 1, n)], pair_ring, k, n)
            for dx in range(2):
                needs = [(k, "in", 3 if n < PIECES // 2 else 1, dx, n)]
                if dx == 1 and n in VIA_PAIR[k]:
                    needs = [(k, "in", 2, 0, n)]
                task((k, "on", n, dx), needs, onward, k, dx, n)
        task((k, "swap", 0, 0, "!"), [], own_swap, k)
        for dr in range(4):
            for dx in range(2):
                needs = [(k, "in", dr, dx, n) for n in range(PIECES)] if dr + dx else []
                if needs:
                    task((k, "swap", dr, dx, "!"), needs, swap, k, dr, dx)
                task((k, "dot", dr, dx), ["load", (k, "swap", dr, dx)] + needs, partial, k, dr, dx)

    def ways(p):
        h = p // 2
        return h, 1 + 2 * h, 3 - 2 * h

    def spread(k, dr, dx):
        c = chains[k]
        p, i = spot(k, dr, dx)
        h, way, back = ways(p)
        far = (dr, dx) in FAR_SUM
        if far:
            send((k, "c", dr, dx), c["ms"].at[way, p, i], c["rb"].at[h, p, i], c["second"].to(way))
        send((k, "a", dr, dx), c["ms"].at[2, p, i], c["ra"].at[p, i], c["second"].to(2 if far else way))
        send((k, "b", dr, dx), c["ms"].at[back, p, i], c["rb"].at[1 - h, p, i], c["second"].to(back))

    def join(k, dr, dx):
        c = chains[k]
        p, i = spot(k, dr, dx)
        h, way, _ = ways(p)
        c["ms"][way, p, i] = encode(c["pf"][way, p, i] + decode(c["ra"][p, i]))
        send((k, "c", dr, dx), c["ms"].at[way, p, i], c["rb"].at[h, p, i], c["second"].to(way))

    def finish(k, dr, dx):
        c = chains[k]
        p, i = spot(k, dr, dx)
        total = c["pf"][0, p, i] + (decode(c["rb"][0, p, i]) + decode(c["rb"][1, p, i]))
        if (dr, dx) in FAR_SUM:
            total += decode(c["ra"][p, i])
        c["mx"][p, i] = encode(total)
        send((k, "x", dr, dx), c["mx"].at[p, i], c["rx"].at[p, i], c["second"].to(0, 1))
        c["pf"][0, p, i] = total

    def region(k, dr, dx, away):
        p, i = spot(k, dr, dx)
        full = full_a if k == "a" else full_g.at[core]
        return full.at[p, i, lax.rem(chains[k]["second"].ring + away, 4)]

    def rounded(k, dr, dx):
        c = chains[k]
        place = c["second"]
        p, i = spot(k, dr, dx)
        _, way, back = ways(p)
        for x in range(2):
            own = lax.rem(place.pair + x, 2)
            value = (c["pf"][0, p, i, x] + decode(c["rx"][p, i, 1 - x])).astype(BF16)
            if k == "a":
                full_a[p, i, place.ring, own] = value
            else:
                full_g[core, p, i, place.ring, own] = value
        mine = region(k, dr, dx, 0)
        send((k, "r", dr, dx), mine, mine, place.to(way))
        send((k, "s", dr, dx), mine, mine, place.to(back))
        if (dr, dx) in FAR_OUT:
            send((k, "f", dr, dx), mine, mine, place.to(2))

    def onward_rounded(k, dr, dx):
        _, way, back = ways(spot(k, dr, dx)[0])
        there = region(k, dr, dx, back)
        send((k, "f", dr, dx), there, there, chains[k]["second"].to(way))

    def share(dr, dx, n):
        _, way, back = ways(spot("g", dr, dx)[0])
        there = region("g", dr, dx, (0, back, way, 2)[n])
        send(("t", n, dr, dx), there, there, sibling)

    def leave(k, dr, dx):
        p, i = spot(k, dr, dx)
        if k == "a":
            local(full_a.at[p, i], out_a.at[p, i])
        else:
            for n in range(2):
                local(full_g.at[n, p, i], out_g.at[n, p, i])

    for k in "ga":
        for dr in range(4):
            for dx in range(2):
                at = (dr, dx)
                task((k, "spread") + at, [(k, "dot") + at], spread, k, dr, dx)
                sums = [(k, "b") + at, (k, "c") + at]
                if at in FAR_SUM:
                    sums.append((k, "a") + at)
                else:
                    task((k, "join") + at, [(k, "a") + at], join, k, dr, dx)
                task((k, "end") + at, sums, finish, k, dr, dx)
                task((k, "round") + at, [(k, "x") + at], rounded, k, dr, dx)
                if at not in FAR_OUT:
                    task((k, "pass") + at, [(k, "r") + at], onward_rounded, k, dr, dx)
                arrivals = [(k, "r") + at, (k, "s") + at, (k, "f") + at]
                needs = [(k, "round") + at] + arrivals
                if k == "g":
                    for n in range(4):
                        task(("share", n) + at, [needs[n]], share, dr, dx, n)
                        needs.append(("t", n) + at)
                task((k, "leave") + at, needs, leave, k, dr, dx)

    run_tasks(tasks, copies, got)
    for copy in locals_[len(loads):]:
        copy.wait()
    for copy in sent:
        copy.wait_send()


def rotate(acts, grads, act_basis, grad_basis):
    any_space = pl.BlockSpec(memory_space=pl.ANY)
    shape = (4, 2, 4, 2, 32, 512)
    per_chain = lambda *dims, dtype=BF16: [pltpu.VMEM(dims, dtype)] * 2
    return pl.pallas_call(
        exchange_kernel,
        out_shape=(jax.ShapeDtypeStruct(shape, BF16), jax.ShapeDtypeStruct((2,) + shape, BF16)),
        in_specs=[any_space] * 4,
        out_specs=(any_space, any_space),
        scratch_shapes=[
            pltpu.VMEM((4, 2, 2, 128, 1024), BF16),
            pltpu.VMEM((4, 2, 2, 256, 512), BF16),
            pltpu.VMEM((1024, 512), BF16),
            pltpu.VMEM((2, 512, 512), BF16),
            *per_chain(4, 4, 2, 2, 32, 512, dtype=F32),
            *per_chain(4, 4, 2, 2, 32, 512),
            *per_chain(4, 2, 2, 32, 512),
            *per_chain(2, 4, 2, 2, 32, 512),
            *per_chain(4, 2, 2, 32, 512),
            *per_chain(4, 2, 2, 32, 512),
            pltpu.VMEM(shape, BF16),
            pltpu.VMEM((2,) + shape, BF16),
            pltpu.SemaphoreType.DMA((260,)),
            pltpu.SemaphoreType.DMA((260,)),
            pltpu.SemaphoreType.DMA((32,)),
        ],
        compiler_params=pltpu.CompilerParams(collective_id=0, has_side_effects=True, vmem_limit_bytes=60 << 20),
        cost_estimate=pl.CostEstimate(flops=4 * 2048 * 1024 * 512, bytes_accessed=10 << 20, transcendentals=0),
    )(acts, grads, act_basis, grad_basis)


ALIGN = 16
CHUNK = 512


def tiles_kernel(lengths, order, ra_hbm, rg_hbm, out, ra, rg, sems):
    def chunk(n):
        rows = pl.ds(pl.multiple_of(n * CHUNK, CHUNK), CHUNK)
        return [pltpu.make_async_copy(ra_hbm.at[rows], ra.at[rows], sems.at[n, 0])] + [
            pltpu.make_async_copy(rg_hbm.at[h, rows], rg.at[rows, pl.ds(h * 512, 512)], sems.at[n, 1 + h])
            for h in range(2)
        ]

    for n in range(TOTAL // CHUNK):
        for copy in chunk(n):
            copy.start()
    out[...] = jnp.zeros_like(out)

    @pl.loop(0, SEQS, init_carry=(jnp.int32(0), jnp.int32(0)))
    def _(k, carry):
        start, here = carry
        end = start + lengths[order[k]]
        low = start // ALIGN * ALIGN
        size = (end - low + 255) // 256 * 256
        low = jnp.minimum(low, TOTAL - size)
        needed = (low + size + CHUNK - 1) // CHUNK

        @pl.loop(here, needed)
        def _(n):
            for copy in chunk(n):
                copy.wait()

        def add(rows):
            at = pl.multiple_of(low, ALIGN)
            token = at + lax.broadcasted_iota(jnp.int32, (rows, 1), 0)
            a = jnp.where((token >= start) & (token < end), ra[pl.ds(at, rows)], 0)
            tile = lax.dot_general(rg[pl.ds(at, rows)], a, (((0,), (0,)), ((), ())), preferred_element_type=F32)
            out[...] += tile * (tile * (1.0 / TOTAL))

        lax.switch(size // 256 - 1, [functools.partial(add, rows) for rows in (256, 512, 768)])
        return end, jnp.maximum(here, needed)


def tiles(lengths, order, ra, rg):
    smem, anywhere = pl.BlockSpec(memory_space=pltpu.SMEM), pl.BlockSpec(memory_space=pl.ANY)
    return pl.pallas_call(
        tiles_kernel,
        out_shape=jax.ShapeDtypeStruct((1024, 512), F32),
        in_specs=[smem, smem, anywhere, anywhere],
        out_specs=pl.BlockSpec(memory_space=pltpu.VMEM),
        scratch_shapes=[
            pltpu.VMEM((TOTAL, 512), BF16),
            pltpu.VMEM((TOTAL, 1024), BF16),
            pltpu.SemaphoreType.DMA((TOTAL // CHUNK, 3)),
        ],
        compiler_params=pltpu.CompilerParams(vmem_limit_bytes=60 << 20),
    )(lengths, order, ra, rg)


def shards(activations, gradients, act_basis, grad_basis, lengths, seq_order):
    ra, rg = rotate(activations, gradients, act_basis, grad_basis)
    return tiles(lengths, seq_order, ra.reshape(2048, 512), rg.reshape(2, 2048, 512))


def solution(mesh):
    in_specs = (P("col", "row"), P("row", "col"), P("row", "col"), P("col", "row"), P(), P())
    return jax.shard_map(shards, mesh=mesh, in_specs=in_specs, out_specs=P("row", "col"), check_vma=False)
```

```python
import functools

import jax
import jax.numpy as jnp
from jax import lax
from jax.experimental import pallas as pl
from jax.experimental.pallas import tpu as pltpu
from jax.sharding import PartitionSpec as P

MESH = pl.DeviceIdType.MESH
SEQS = 8
TOTAL = 2048
SCALE = 2.0**40
TINY = 2.0**-126

PIECES = 4
VIA_PAIR = {"a": (0, 1, 2, 3), "g": (0, 1, 2, 3)}
IN_FLIGHT = 60
FAR_SUM = ()
FAR_OUT = ()
ORDER = (
    7, 43, 13, 49, 39, 3, 8, 44, 18, 54, 12, 48, 2, 38, 53, 17, 22, 58, 0, 10, 15, 46, 51, 14, 1, 23, 50, 74, 59,
    56, 41, 20, 5, 154, 40, 34, 70, 62, 26, 4, 11, 16, 52, 47, 9, 35, 134, 45, 71, 6, 21, 30, 75, 190, 63, 19, 27,
    57, 42, 155, 66, 24, 94, 55, 60, 166, 31, 114, 135, 67, 178, 25, 84, 191, 61, 160, 36, 28, 76, 156, 95, 64, 37,
    144, 167, 115, 32, 72, 179, 29, 192, 136, 104, 65, 172, 85, 161, 68, 33, 124, 96, 73, 196, 77, 168, 79, 145,
    180, 157, 116, 69, 184, 105, 173, 193, 86, 137, 162, 125, 139, 197, 97, 99, 81, 78, 80, 169, 158, 146, 106, 185,
    181, 138, 141, 194, 140, 117, 119, 174, 126, 198, 87, 98, 89, 100, 101, 82, 163, 170, 186, 147, 142, 149, 159,
    83, 121, 182, 107, 118, 120, 109, 88, 90, 143, 195, 175, 91, 164, 102, 127, 129, 148, 150, 151, 171, 199, 183,
    103, 111, 108, 110, 187, 176, 92, 122, 165, 128, 131, 130, 93, 123, 200, 152, 112, 188, 153, 177, 113, 132, 201,
    133, 189,
)

BF16, F32 = jnp.bfloat16, jnp.float32


def encode(v):
    v = v * SCALE
    size = jnp.abs(v)
    return (v * (size * jnp.sqrt(size))).astype(BF16)


def decode(m):
    v = m.astype(F32)
    size = jnp.abs(v)
    root = jnp.exp2(jnp.log2(jnp.maximum(size, TINY)) * 0.4) * (1.0 / SCALE)
    root = jnp.where(size >= TINY, root, 0.0)
    return jnp.where(v < 0, -root, root)


def run_tasks(tasks, copies, got):
    steps, done = list(tasks.items()), set()
    for n in ORDER:
        key, (needs, step) = steps[n]
        for name in needs:
            if name in copies:
                got(name)
            else:
                assert name in done
        step()
        done.add(key)
    assert len(done) == len(steps)


class Place:
    def __init__(self, ring, pair, peer):
        self.ring, self.pair, self.peer = ring, pair, peer

    def to(self, dr=0, dx=0):
        return self.peer(lax.rem(self.ring + dr + 4, 4), lax.rem(self.pair + dx, 2))

    def index(self, dr=0, dx=0):
        return lax.rem(self.ring + dr + 4, 4) * 2 + lax.rem(self.pair + dx, 2)


def exchange_kernel(
    acts, grads, act_basis, grad_basis, out_a, out_g,
    ga, gg, ba, bg, pf_a, pf_g, ms_a, ms_g, ra_a, ra_g, rb_a, rb_g, mx_a, mx_g, rx_a, rx_g, full_a, full_g,
    send_sems, recv_sems, local_sems,
):
    row, col = lax.axis_index("row"), lax.axis_index("col")
    y, xh = row // 2, lax.rem(row, 2)
    z, xl, core = col // 4, lax.rem(col // 2, 2), lax.rem(col, 2)
    other = 1 - core
    along_z = Place(z, xl, lambda r, p: (row, r * 4 + p * 2 + core))
    along_y = Place(y, xh, lambda r, p: (r * 2 + p, col))
    sibling = (row, z * 4 + xl * 2 + other)

    copies, waited, sent, locals_, tasks = {}, set(), [], [], {}

    def send(name, src, dst, to):
        n = len(copies)
        copy = pltpu.make_async_remote_copy(
            src_ref=src, dst_ref=dst, send_sem=send_sems.at[n], recv_sem=recv_sems.at[n],
            device_id=to, device_id_type=MESH,
        )
        copies[name] = copy
        copy.start()
        sent.append(copy)
        if len(sent) > IN_FLIGHT:
            sent.pop(0).wait_send()

    def got(name):
        if name not in waited:
            waited.add(name)
            copies[name].wait_recv()

    def local(src, dst):
        copy = pltpu.make_async_copy(src, dst, local_sems.at[len(locals_)])
        locals_.append(copy)
        copy.start()
        return copy

    def task(key, needs, step, *args):
        tasks[key] = (needs, functools.partial(step, *args))

    partners = [along_z.to(1), along_z.to(3), along_z.to(0, 1), along_y.to(1), along_y.to(3), along_y.to(0, 1), sibling]
    if FAR_SUM or FAR_OUT:
        partners += [along_z.to(2), along_y.to(2)]
    barrier = pltpu.get_barrier_semaphore()
    for partner in partners:
        pl.semaphore_signal(barrier, inc=1, device_id=partner, device_id_type=MESH)
    loads = [local(acts, ga.at[0, 0, core]), local(grads, gg.at[0, 0, core]), local(act_basis, ba)]
    half_of = lambda who: pl.ds(pl.multiple_of(who * 512, 512), 512)
    loads.append(local(grad_basis.at[:, half_of(core)], bg.at[core]))
    pl.semaphore_wait(barrier, len(partners))

    chains = {
        "a": dict(mine=acts, g=ga, first=along_z, second=along_y, pf=pf_a, ms=ms_a, ra=ra_a, rb=rb_a, mx=mx_a, rx=rx_a),
        "g": dict(mine=grads, g=gg, first=along_y, second=along_z, pf=pf_g, ms=ms_g, ra=ra_g, rb=rb_g, mx=mx_g, rx=rx_g),
    }

    def loaded():
        for copy in loads:
            copy.wait()

    def basis():
        send("basis", grad_basis.at[:, half_of(other)], bg.at[core], sibling)

    task("swap", [], basis)
    task("load", ["basis"], loaded)

    def piece(k, n):
        rows = (128 if k == "a" else 256) // PIECES
        return pl.ds(n * rows, rows)

    def own_ring(k, n):
        c = chains[k]
        mine, g, place = c["mine"], c["g"], c["first"]
        rows = piece(k, n)
        send((k, "in", 3, 0, n), mine.at[rows], g.at[3, 0, core, rows], place.to(1))
        n = PIECES - 1 - n
        rows = piece(k, n)
        send((k, "in", 1, 0, n), mine.at[rows], g.at[1, 0, core, rows], place.to(3))

    def own_pair(k, n):
        c = chains[k]
        rows = piece(k, n)
        send((k, "in", 0, 1, n), c["mine"].at[rows], c["g"].at[0, 1, core, rows], c["first"].to(0, 1))

    def own_swap(k):
        c = chains[k]
        send((k, "swap", 0, 0), c["mine"], c["g"].at[0, 0, core], sibling)

    def swap(k, dr, dx):
        g = chains[k]["g"]
        send((k, "swap", dr, dx), g.at[dr, dx, core], g.at[dr, dx, core], sibling)

    def pair_ring(k, n):
        g, place = chains[k]["g"], chains[k]["first"]
        rows = piece(k, n)
        send((k, "in", 3, 1, n), g.at[0, 1, core, rows], g.at[3, 1, core, rows], place.to(1))
        send((k, "in", 1, 1, n), g.at[0, 1, core, rows], g.at[1, 1, core, rows], place.to(3))

    def onward(k, dx, n):
        g, place = chains[k]["g"], chains[k]["first"]
        rows = piece(k, n)
        if dx == 1 and n in VIA_PAIR[k]:
            send((k, "in", 2, 1, n), g.at[2, 0, core, rows], g.at[2, 1, core, rows], place.to(0, 1))
            return
        dr = 1 if n < PIECES // 2 else 3
        send((k, "in", 2, dx, n), g.at[4 - dr, dx, core, rows], g.at[2, dx, core, rows], place.to(dr))

    def spot(k, dr, dx):
        first = chains[k]["first"]
        return lax.rem(first.ring + dr, 4), lax.rem(first.pair + dx, 2)

    def partial(k, dr, dx):
        c = chains[k]
        second, g = c["second"], c["g"]
        p, i = spot(k, dr, dx)

        def keep(value, base):
            for s in range(value.shape[0] // 32):
                o = base + s
                q = lax.rem(o // 2 - second.ring + 4, 4)
                x = lax.rem(o % 2 + second.pair, 2)
                piece = value[s * 32 : (s + 1) * 32]
                c["pf"][q, p, i, x] = piece
                c["ms"][q, p, i, x] = encode(piece)

        for n in range(2):
            if k == "a":
                value = jnp.dot(g[dr, dx, n], ba[...], preferred_element_type=F32)
            else:
                rows = pl.ds(n * 128, 128)
                value = jnp.dot(g[dr, dx, 0, rows], bg[0], preferred_element_type=F32)
                value += jnp.dot(g[dr, dx, 1, rows], bg[1], preferred_element_type=F32)
            keep(value, 4 * n)

    for k in "ga":
        for n in range(PIECES):
            task((k, "own", n), [], own_ring, k, n)
            task((k, "pair", n), [], own_pair, k, n)
            task((k, "ring", n), [(k, "in", 0, 1, n)], pair_ring, k, n)
            for dx in range(2):
                needs = [(k, "in", 3 if n < PIECES // 2 else 1, dx, n)]
                if dx == 1 and n in VIA_PAIR[k]:
                    needs = [(k, "in", 2, 0, n)]
                task((k, "on", n, dx), needs, onward, k, dx, n)
        task((k, "swap", 0, 0, "!"), [], own_swap, k)
        for dr in range(4):
            for dx in range(2):
                needs = [(k, "in", dr, dx, n) for n in range(PIECES)] if dr + dx else []
                if needs:
                    task((k, "swap", dr, dx, "!"), needs, swap, k, dr, dx)
                task((k, "dot", dr, dx), ["load", (k, "swap", dr, dx)] + needs, partial, k, dr, dx)

    def ways(p):
        h = p // 2
        return h, 1 + 2 * h, 3 - 2 * h

    def spread(k, dr, dx):
        c = chains[k]
        p, i = spot(k, dr, dx)
        h, way, back = ways(p)
        far = (dr, dx) in FAR_SUM
        if far:
            send((k, "c", dr, dx), c["ms"].at[way, p, i], c["rb"].at[h, p, i], c["second"].to(way))
        send((k, "a", dr, dx), c["ms"].at[2, p, i], c["ra"].at[p, i], c["second"].to(2 if far else way))
        send((k, "b", dr, dx), c["ms"].at[back, p, i], c["rb"].at[1 - h, p, i], c["second"].to(back))

    def join(k, dr, dx):
        c = chains[k]
        p, i = spot(k, dr, dx)
        h, way, _ = ways(p)
        c["ms"][way, p, i] = encode(c["pf"][way, p, i] + decode(c["ra"][p, i]))
        send((k, "c", dr, dx), c["ms"].at[way, p, i], c["rb"].at[h, p, i], c["second"].to(way))

    def finish(k, dr, dx):
        c = chains[k]
        p, i = spot(k, dr, dx)
        total = c["pf"][0, p, i] + (decode(c["rb"][0, p, i]) + decode(c["rb"][1, p, i]))
        if (dr, dx) in FAR_SUM:
            total += decode(c["ra"][p, i])
        c["mx"][p, i] = encode(total)
        send((k, "x", dr, dx), c["mx"].at[p, i], c["rx"].at[p, i], c["second"].to(0, 1))
        c["pf"][0, p, i] = total

    def region(k, dr, dx, away):
        p, i = spot(k, dr, dx)
        full = full_a if k == "a" else full_g.at[core]
        return full.at[p, i, lax.rem(chains[k]["second"].ring + away, 4)]

    def rounded(k, dr, dx):
        c = chains[k]
        place = c["second"]
        p, i = spot(k, dr, dx)
        _, way, back = ways(p)
        for x in range(2):
            own = lax.rem(place.pair + x, 2)
            value = (c["pf"][0, p, i, x] + decode(c["rx"][p, i, 1 - x])).astype(BF16)
            if k == "a":
                full_a[p, i, place.ring, own] = value
            else:
                full_g[core, p, i, place.ring, own] = value
        mine = region(k, dr, dx, 0)
        send((k, "r", dr, dx), mine, mine, place.to(way))
        send((k, "s", dr, dx), mine, mine, place.to(back))
        if (dr, dx) in FAR_OUT:
            send((k, "f", dr, dx), mine, mine, place.to(2))

    def onward_rounded(k, dr, dx):
        _, way, back = ways(spot(k, dr, dx)[0])
        there = region(k, dr, dx, back)
        send((k, "f", dr, dx), there, there, chains[k]["second"].to(way))

    def share(dr, dx, n):
        _, way, back = ways(spot("g", dr, dx)[0])
        there = region("g", dr, dx, (0, back, way, 2)[n])
        send(("t", n, dr, dx), there, there, sibling)

    def leave(k, dr, dx):
        p, i = spot(k, dr, dx)
        if k == "a":
            local(full_a.at[p, i], out_a.at[p, i])
        else:
            for n in range(2):
                local(full_g.at[n, p, i], out_g.at[n, p, i])

    for k in "ga":
        for dr in range(4):
            for dx in range(2):
                at = (dr, dx)
                task((k, "spread") + at, [(k, "dot") + at], spread, k, dr, dx)
                sums = [(k, "b") + at, (k, "c") + at]
                if at in FAR_SUM:
                    sums.append((k, "a") + at)
                else:
                    task((k, "join") + at, [(k, "a") + at], join, k, dr, dx)
                task((k, "end") + at, sums, finish, k, dr, dx)
                task((k, "round") + at, [(k, "x") + at], rounded, k, dr, dx)
                if at not in FAR_OUT:
                    task((k, "pass") + at, [(k, "r") + at], onward_rounded, k, dr, dx)
                arrivals = [(k, "r") + at, (k, "s") + at, (k, "f") + at]
                needs = [(k, "round") + at] + arrivals
                if k == "g":
                    for n in range(4):
                        task(("share", n) + at, [needs[n]], share, dr, dx, n)
                        needs.append(("t", n) + at)
                task((k, "leave") + at, needs, leave, k, dr, dx)

    run_tasks(tasks, copies, got)
    for copy in locals_[len(loads):]:
        copy.wait()
    for copy in sent:
        copy.wait_send()


def rotate(acts, grads, act_basis, grad_basis):
    any_space = pl.BlockSpec(memory_space=pl.ANY)
    shape = (4, 2, 4, 2, 32, 512)
    per_chain = lambda *dims, dtype=BF16: [pltpu.VMEM(dims, dtype)] * 2
    return pl.pallas_call(
        exchange_kernel,
        out_shape=(jax.ShapeDtypeStruct(shape, BF16), jax.ShapeDtypeStruct((2,) + shape, BF16)),
        in_specs=[any_space] * 4,
        out_specs=(any_space, any_space),
        scratch_shapes=[
            pltpu.VMEM((4, 2, 2, 128, 1024), BF16),
            pltpu.VMEM((4, 2, 2, 256, 512), BF16),
            pltpu.VMEM((1024, 512), BF16),
            pltpu.VMEM((2, 512, 512), BF16),
            *per_chain(4, 4, 2, 2, 32, 512, dtype=F32),
            *per_chain(4, 4, 2, 2, 32, 512),
            *per_chain(4, 2, 2, 32, 512),
            *per_chain(2, 4, 2, 2, 32, 512),
            *per_chain(4, 2, 2, 32, 512),
            *per_chain(4, 2, 2, 32, 512),
            pltpu.VMEM(shape, BF16),
            pltpu.VMEM((2,) + shape, BF16),
            pltpu.SemaphoreType.DMA((260,)),
            pltpu.SemaphoreType.DMA((260,)),
            pltpu.SemaphoreType.DMA((32,)),
        ],
        compiler_params=pltpu.CompilerParams(collective_id=0, has_side_effects=True, vmem_limit_bytes=60 << 20),
        cost_estimate=pl.CostEstimate(flops=4 * 2048 * 1024 * 512, bytes_accessed=10 << 20, transcendentals=0),
    )(acts, grads, act_basis, grad_basis)


ALIGN = 16
CHUNK = 256
OUT_ROWS = 256


def tiles_kernel(lengths, order, ra_hbm, rg_hbm, out_hbm, out, ra, rg, sems, out_sems):
    def chunk(n):
        rows = pl.ds(pl.multiple_of(n * CHUNK, CHUNK), CHUNK)
        return [pltpu.make_async_copy(ra_hbm.at[rows], ra.at[rows], sems.at[n, 0])] + [
            pltpu.make_async_copy(rg_hbm.at[h, rows], rg.at[rows, pl.ds(h * 512, 512)], sems.at[n, 1 + h])
            for h in range(2)
        ]

    for n in range(TOTAL // CHUNK):
        for copy in chunk(n):
            copy.start()
    out[...] = jnp.zeros_like(out)

    def window(k, start, here):
        end = start + lengths[order[k]]
        low = start // ALIGN * ALIGN
        size = (end - low + 255) // 256 * 256
        low = jnp.minimum(low, TOTAL - size)
        needed = (low + size + CHUNK - 1) // CHUNK

        @pl.loop(here, needed)
        def _(n):
            for copy in chunk(n):
                copy.wait()

        return end, low, size, jnp.maximum(here, needed)

    def add(start, end, low, size, part):
        def some(rows):
            at = pl.multiple_of(low, ALIGN)
            token = at + lax.broadcasted_iota(jnp.int32, (rows, 1), 0)
            a = jnp.where((token >= start) & (token < end), ra[pl.ds(at, rows)], 0)
            tile = lax.dot_general(rg[pl.ds(at, rows), part], a, (((0,), (0,)), ((), ())), preferred_element_type=F32)
            out[part] += tile * (tile * (1.0 / TOTAL))

        lax.switch(size // 256 - 1, [functools.partial(some, rows) for rows in (256, 512, 768)])

    def one(k, carry):
        start, here = carry
        end, low, size, here = window(k, start, here)
        add(start, end, low, size, slice(0, 1024))
        return end, here

    start, here = lax.fori_loop(0, SEQS - 1, one, (jnp.int32(0), jnp.int32(0)))
    end, low, size, _ = window(SEQS - 1, start, here)
    leaving = []
    for n in range(1024 // OUT_ROWS):
        part = slice(n * OUT_ROWS, (n + 1) * OUT_ROWS)
        add(start, end, low, size, part)
        rows = pl.ds(n * OUT_ROWS, OUT_ROWS)
        leaving.append(pltpu.make_async_copy(out.at[rows], out_hbm.at[rows], out_sems.at[n]))
        leaving[-1].start()
    for copy in leaving:
        copy.wait()


def tiles(lengths, order, ra, rg):
    smem, anywhere = pl.BlockSpec(memory_space=pltpu.SMEM), pl.BlockSpec(memory_space=pl.ANY)
    return pl.pallas_call(
        tiles_kernel,
        out_shape=jax.ShapeDtypeStruct((1024, 512), F32),
        in_specs=[smem, smem, anywhere, anywhere],
        out_specs=anywhere,
        scratch_shapes=[
            pltpu.VMEM((1024, 512), F32),
            pltpu.VMEM((TOTAL, 512), BF16),
            pltpu.VMEM((TOTAL, 1024), BF16),
            pltpu.SemaphoreType.DMA((TOTAL // CHUNK, 3)),
            pltpu.SemaphoreType.DMA((1024 // OUT_ROWS,)),
        ],
        compiler_params=pltpu.CompilerParams(vmem_limit_bytes=60 << 20),
    )(lengths, order, ra, rg)


def shards(activations, gradients, act_basis, grad_basis, lengths, seq_order):
    ra, rg = rotate(activations, gradients, act_basis, grad_basis)
    return tiles(lengths, seq_order, ra.reshape(2048, 512), rg.reshape(2, 2048, 512))


def solution(mesh):
    in_specs = (P("col", "row"), P("row", "col"), P("row", "col"), P("col", "row"), P(), P())
    return jax.shard_map(shards, mesh=mesh, in_specs=in_specs, out_specs=P("row", "col"), check_vma=False)
```
